32 devices in a mesh: heads: 2 (over x), team: 2 (over core), blk: 8 (over z, y).
Axes of the slice: x: 2, y: 2, z: 4, core: 2. Of those that a mesh axis runs over, the one named last changes fastest.
Arguments:
- queries: bfloat16 [2, 512, 32, 128], P('heads', ('team', 'blk')), may hold values from -26 to 26
- keys: bfloat16 [2, 512, 8, 128], P('heads', ('team', 'blk')), may hold values from -26 to 26
- values: bfloat16 [2, 512, 8, 128], P('heads', ('team', 'blk')), may hold values from -6 to 6
- run_index: int32 [16], replicated, may hold values from 0 to 15, each once
Outputs:
- attended: bfloat16 [1024, 32, 128], P(('team', 'blk'), 'heads')
The draws below stay inside these ranges and needn't reach their ends.
All inputs are finite; a program needn't handle non-finite values.
Results may differ from the reference program's by a relative error of at most 0.012.
The reference program's roundings to bfloat16 on the way count: a program that leaves them out, or rounds other values in their place, can miss the bound.
Values may be sent and summed in bfloat16 or wider, within the bound.
A program may use at most 64 MiB of HBM per device.

```python
import math
import jax
import jax.numpy as jnp
from jax import lax

HD = 128
QH = 32
KVH = 8
ROW_DEV = 64
SPLITS = 2
PIECE = 32
SLOTS = 16
SEQ = 1024


def draw_queries(key, part):
    shape = (SPLITS, SLOTS * PIECE, QH, HD)
    base = 1.7 * jax.random.normal(jax.random.fold_in(key, 11), shape, jnp.float32)
    return jnp.clip(base, -26.0, 26.0).astype(jnp.bfloat16)


def draw_keys(key, part):
    shape = (SPLITS, SLOTS * PIECE, KVH, HD)
    base = 1.7 * jax.random.normal(jax.random.fold_in(key, 21), shape, jnp.float32)
    return jnp.clip(base, -26.0, 26.0).astype(jnp.bfloat16)


def steps_of(own_key, shape, pieces, smallest, top_value):
    loudness, own = 1.0, jax.random.fold_in(own_key, 6)
    for axis_at, shards_of in pieces:
        heights = jnp.exp(jax.random.uniform(jax.random.fold_in(own, axis_at), (shards_of,), jnp.float32, smallest / len(pieces), top_value / len(pieces)))
        loudness = loudness * jnp.repeat(heights, shape[axis_at] // shards_of).reshape([-1 if axis == axis_at else 1 for axis in range(len(shape))])
    return loudness


def normal_values(own_key, dims, deviation, limit, cuts=(), kind=jnp.bfloat16):
    drawn = deviation * jax.random.normal(own_key, dims, jnp.float32)
    if cuts:
        drawn = drawn * steps_of(own_key, dims, cuts, -0.22, 0.18)
    return jnp.clip(drawn, -limit, limit).astype(kind)


def setup_inputs(seed: int = 0) -> dict:
    key_of = jax.random.split(jax.random.key(seed), 5)
    return {
        "queries": draw_queries(jax.random.fold_in(key_of[4], 71), 0),
        "keys": draw_keys(jax.random.fold_in(key_of[4], 71), 0),
        "values": normal_values(key_of[2], (SPLITS, SLOTS * PIECE, KVH, HD), 1.0, 6.0, ((0, 2), (1, 16))),
        "run_index": jax.random.permutation(key_of[3], SLOTS).astype(jnp.int32),
    }


rope_theta = 500000.0
rope_factor = 8.0
low_factor = 1.0
high_factor = 4.0
initial_context = 8192.0


def inverse_freqs(head_width):
    half_width = head_width // 2
    counter = jnp.arange(half_width, dtype=jnp.float32)
    base_freq = 1.0 / (rope_theta ** (2.0 * counter / head_width))
    wavelength = 2.0 * jnp.pi / base_freq
    smooth = (initial_context / wavelength - low_factor) / (high_factor - low_factor)
    blended = (1.0 - smooth) * base_freq / rope_factor + smooth * base_freq
    middle = jnp.where(wavelength > initial_context / low_factor, base_freq / rope_factor, blended)
    return jnp.where(wavelength < initial_context / high_factor, base_freq, middle)


def rotate_heads(values_in, positions, inverse):
    half_width = values_in.shape[-1] // 2
    angles = positions.astype(jnp.float32)[:, None] * inverse[None, :]
    cosine = jnp.cos(angles)[:, None, :]
    sine_part = jnp.sin(angles)[:, None, :]
    first_half = values_in[..., :half_width]
    second = values_in[..., half_width:]
    return jnp.concatenate([first_half * cosine - second * sine_part, second * cosine + first_half * sine_part], axis=-1)


def slot_order(array):
    heads_here = array.shape[2]
    grid = array.reshape(SPLITS, SLOTS, PIECE, heads_here, HD)
    return jnp.transpose(grid, (1, 0, 2, 3, 4)).reshape(SEQ, heads_here, HD)


def reference(queries, keys, values, run_index):
    all_rows = jnp.arange(SEQ, dtype=jnp.int32)
    slot_ids = all_rows // ROW_DEV
    local_rows = all_rows % ROW_DEV
    run_ids = run_index[slot_ids].astype(jnp.int32)
    half_rows = ROW_DEV // 2
    early_at = run_ids * half_rows + local_rows
    late_at = (2 * SLOTS - 1 - run_ids) * half_rows + local_rows - half_rows
    positions = jnp.where(local_rows < half_rows, early_at, late_at).astype(jnp.int32)
    inverse = inverse_freqs(HD)
    rot_q = rotate_heads(slot_order(queries).astype(jnp.float32), positions, inverse).astype(jnp.bfloat16)
    rot_k = rotate_heads(slot_order(keys).astype(jnp.float32), positions, inverse).astype(jnp.bfloat16)
    ordered_v = slot_order(values)
    group_size = QH // KVH
    scaling = HD ** -0.5
    block_rows = ROW_DEV * math.gcd(SLOTS, max(1, 768 // ROW_DEV))
    block_count = SEQ // block_rows
    grouped_q = rot_q.reshape(block_count, block_rows, KVH, group_size, HD)
    pos_blocks = positions.reshape(block_count, block_rows)

    def attend_block(packed):
        query_block, query_pos = packed
        visible = (positions[None, :] <= query_pos[:, None])[None]

        def per_head(head_id):
            head_q = lax.dynamic_index_in_dim(query_block, head_id, 1, keepdims=False).astype(jnp.float32)
            head_k = lax.dynamic_index_in_dim(rot_k, head_id, 1, keepdims=False).astype(jnp.float32)
            head_v = lax.dynamic_index_in_dim(ordered_v, head_id, 1, keepdims=False).astype(jnp.float32)
            scores = jnp.einsum("bgd,kd->gbk", head_q, head_k) * scaling
            scores = jnp.where(visible, scores, -jnp.inf)
            highest = jnp.max(scores, axis=-1, keepdims=True)
            weights = jnp.exp(scores - highest)
            denominator = jnp.sum(weights, axis=-1)
            rounded = lax.optimization_barrier(weights.astype(jnp.bfloat16)).astype(jnp.float32)
            mixed = jnp.einsum("gbk,kd->gbd", rounded, head_v)
            return mixed / denominator[..., None]

        per_group = lax.map(per_head, jnp.arange(KVH, dtype=jnp.int32))
        return jnp.transpose(per_group, (2, 0, 1, 3)).reshape(block_rows, QH, HD)

    attended = lax.map(attend_block, (grouped_q, pos_blocks))
    return attended.reshape(SEQ, QH, HD).astype(jnp.bfloat16)
```

```python
import functools
import math

import jax
import jax.numpy as jnp
import numpy as np
from jax import lax
from jax.experimental import pallas as pl
from jax.experimental.pallas import tpu as pltpu
from jax.sharding import PartitionSpec as P

mask_floor = -1e30
rope_theta = 500000.0
rope_factor = 8.0
low_factor = 1.0
high_factor = 4.0
initial_context = 8192.0


def inverse_freqs(head_width):
    counter = np.arange(head_width // 2, dtype=np.float64)
    base_freq = 1.0 / rope_theta ** (2.0 * counter / head_width)
    wavelength = 2.0 * np.pi / base_freq
    smooth = (initial_context / wavelength - low_factor) / (high_factor - low_factor)
    blended = (1.0 - smooth) * base_freq / rope_factor + smooth * base_freq
    middle = np.where(wavelength > initial_context / low_factor, base_freq / rope_factor, blended)
    return np.where(wavelength < initial_context / high_factor, base_freq, middle)


def small_loop(first, last, body):
    if last - first <= 4:
        for at in range(first, last):
            body(at)
    else:
        lax.fori_loop(first, last, lambda at, unused: (body(at), unused)[1], 0)


def attend_kernel(
    dims,
    run_ref,
    freq_ref,
    q_ref,
    k_ref,
    v_ref,
    out_ref,
    kv_out,
    q_out,
    kv_all,
    q_all,
    acc_ref,
    max_ref,
    sum_ref,
    out_part,
    kv_send,
    kv_recv,
    q_send,
    q_recv,
    z_send,
    z_recv,
    y_send,
    y_recv,
    o_send,
    o_recv,
):
    X, C, Z, Y, R, KVL, G, D = dims
    S = C * Z * Y
    half = X * R // 2
    rows = C * G * R
    x, c, b = lax.axis_index("heads"), lax.axis_index("team"), lax.axis_index("blk")
    z, y = b // Y, b % Y
    mine = x * C + c
    power_of_two = Z & (Z - 1) == 0

    def z_to(k):
        if power_of_two and isinstance(k, int):
            at, bit = 0, 1
            while bit < Z:
                at = at + (z // bit + k // bit) % 2 * bit
                bit *= 2
            return at
        return (z + k) % Z

    def z_from(k):
        if power_of_two and isinstance(k, int):
            return z_to(k)
        return (z + Z - k) % Z

    def y_to(m):
        return (y + m) % Y

    def y_from(m):
        return (y + Y - m) % Y

    def device(xx, cc, bb):
        return {"heads": xx, "team": cc, "blk": bb}

    offsets = [(dx, dc) for dx in range(X) for dc in range(C) if (dx, dc) != (0, 0)]

    barrier = pltpu.get_barrier_semaphore()

    def greet(xx, cc, bb):
        pl.semaphore_signal(
            barrier, inc=1, device_id=device(xx, cc, bb), device_id_type=pl.DeviceIdType.MESH
        )

    for dx, dc in offsets:
        greet((x + dx) % X, (c + dc) % C, b)
    small_loop(1, Z, lambda k: greet(x, c, z_to(k) * Y + y))
    small_loop(1, Y, lambda m: greet(x, c, z * Y + y_to(m)))

    def first_pos(slot, piece):
        run = run_ref[slot]
        start = piece * R
        if isinstance(piece, int):
            return run * half + start if start < half else (2 * S - 1 - run) * half + start - half
        return jnp.where(start < half, run * half, (2 * S - 1 - run) * half - half) + start

    own_first = first_pos(c * (Z * Y) + b, x)
    pos = own_first + lax.broadcasted_iota(jnp.int32, (R, D), 0)
    angles = pos.astype(jnp.float32) * freq_ref[...]
    cosine = jnp.cos(angles)
    sine = jnp.sin(angles)
    lanes = lax.broadcasted_iota(jnp.int32, (R, D), 1)
    sine = jnp.where(lanes < D // 2, -sine, sine)

    def by_head(ref, first, count):
        return jnp.swapaxes(ref[0, :, first : first + count, :].astype(jnp.float32), 0, 1)

    def rotated(values):
        turned = pltpu.roll(values, D // 2, 2)
        return values * cosine[None] + turned * sine[None]

    kv_heads = X * C * KVL
    kv_out[:, 0] = (
        rotated(by_head(k_ref, 0, kv_heads)).astype(jnp.bfloat16).reshape(X * C, KVL, R, D)
    )
    kv_out[:, 1] = by_head(v_ref, 0, kv_heads).astype(jnp.bfloat16).reshape(X * C, KVL, R, D)
    kv_all[0, 0, x, :, :, c] = kv_out[mine]

    pl.semaphore_wait(barrier, len(offsets) + Z - 1 + Y - 1)

    def remote(src, dst, send, recv, to):
        return pltpu.make_async_remote_copy(
            src_ref=src,
            dst_ref=dst,
            send_sem=send,
            recv_sem=recv,
            device_id=to,
            device_id_type=pl.DeviceIdType.MESH,
        )

    def kv_copy(dx, dc):
        xx, cc = (x + dx) % X, (c + dc) % C
        return remote(
            kv_out.at[xx * C + cc],
            kv_all.at[0, 0, x, :, :, c],
            kv_send.at[dx, dc],
            kv_recv.at[dx, dc],
            device(xx, cc, b),
        )

    def q_copy(dx, dc):
        xx, cc = (x + dx) % X, (c + dc) % C
        return remote(
            q_out.at[xx * C + cc],
            q_all.at[x, :, c],
            q_send.at[dx, dc],
            q_recv.at[dx, dc],
            device(xx, cc, b),
        )

    for dx, dc in offsets:
        kv_copy(dx, dc).start()

    q_heads = KVL * G
    for to in range(X * C):
        q_out[to] = (
            rotated(by_head(q_ref, to * q_heads, q_heads))
            .astype(jnp.bfloat16)
            .reshape(KVL, G, R, D)
        )
    q_all[x, :, c] = q_out[mine]
    for dx, dc in offsets:
        q_copy(dx, dc).start()

    def z_copy(k, piece):
        return remote(
            kv_all.at[0, 0, piece],
            kv_all.at[k, 0, piece],
            z_send.at[k, piece],
            z_recv.at[k, piece],
            device(x, c, z_to(k) * Y + y),
        )

    def y_copy(k, m, piece):
        return remote(
            kv_all.at[k, 0, piece],
            kv_all.at[k, m, piece],
            y_send.at[k, m, piece],
            y_recv.at[k, m, piece],
            device(x, c, z * Y + y_to(m)),
        )

    def piece_at(dx):
        return (x + X - dx) % X

    for dx in range(X):
        for dc in range(C):
            if (dx, dc) != (0, 0):
                kv_copy(dx, dc).wait_recv()
        piece = piece_at(dx)
        small_loop(1, Z, lambda k: z_copy(k, piece).start())
        small_loop(1, Y, lambda m: y_copy(0, m, piece).start())

    def pass_on(k):
        for dx in range(X):
            piece = piece_at(dx)
            z_copy(k, piece).wait_recv()
            small_loop(1, Y, lambda m: y_copy(k, m, piece).start())

    scaling = math.log2(math.e) * D ** (-0.5)

    def key_positions(k, pieces):
        count = len(pieces) * Y * C * R
        lane = lax.broadcasted_iota(jnp.int32, (1, count), 1)
        segment = lane // R
        total = lane % R
        at = 0
        for piece in pieces:
            for m in range(Y):
                for t in range(C):
                    slot = t * (Z * Y) + z_from(k) * Y + y_from(m)
                    total = total + jnp.where(segment == at, first_pos(slot, piece), 0)
                    at += 1
        return total

    def query_positions(piece):
        row = lax.broadcasted_iota(jnp.int32, (rows, 1), 0)
        total = row % R
        for t in range(C):
            total = total + jnp.where(row // (G * R) == t, first_pos(t * (Z * Y) + b, piece), 0)
        return total

    early = list(range(X // 2))
    late = list(range(X // 2, X))

    def attend(k, first):
        def units(kind, head, pieces):
            return jnp.concatenate(
                [kv_all[k, m, p, kind, head].reshape(C * R, D) for p in pieces for m in range(Y)],
                axis=0,
            )

        key_pos = {"early": key_positions(k, early), "late": key_positions(k, late)}
        for head in range(KVL):
            keys = {"early": units(0, head, early), "late": units(0, head, late)}
            values = {"early": units(1, head, early), "late": units(1, head, late)}
            for piece in range(X):
                query = q_all[piece, head].reshape(rows, D)
                query_pos = query_positions(piece)
                own = "early" if piece in early else "late"
                parts = ["early"] if own == "early" else ["early", "late"]
                scores = []
                for part in parts:
                    s = lax.dot_general(
                        query, keys[part], (((1,), (1,)), ((), ())),
                        preferred_element_type=jnp.float32,
                    )
                    if part == own:
                        s = jnp.where(key_pos[part] <= query_pos, s, mask_floor)
                    scores.append(s)
                top = functools.reduce(
                    jnp.maximum, [jnp.max(s, axis=-1, keepdims=True) for s in scores]
                )
                if not first:
                    before = max_ref[piece, head]
                    top = jnp.maximum(top, before)
                    factor = jnp.exp2((before - top) * scaling)
                weights = [jnp.exp2((s - top) * scaling) for s in scores]
                total = sum(jnp.sum(w, axis=-1, keepdims=True) for w in weights)
                update = sum(
                    jnp.dot(
                        w.astype(jnp.bfloat16), values[part], preferred_element_type=jnp.float32
                    )
                    for w, part in zip(weights, parts)
                )
                if not first:
                    total = total + sum_ref[piece, head] * factor
                    update = update + acc_ref[piece, head] * factor
                max_ref[piece, head] = top
                sum_ref[piece, head] = total
                acc_ref[piece, head] = update


    if Z > 1:
        pass_on(1)
    for dx, dc in offsets:
        q_copy(dx, dc).wait_recv()

    def arrive(k):
        for dx in range(X):
            piece = piece_at(dx)
            small_loop(1, Y, lambda m: y_copy(k, m, piece).wait_recv())

    arrive(0)
    attend(0, True)

    def later(k):
        if isinstance(k, int):
            if k + 1 < Z:
                pass_on(k + 1)
        else:
            pl.when(k + 1 < Z)(lambda: pass_on(k + 1))
        arrive(k)
        attend(k, False)

    small_loop(1, Z, later)

    def o_copy(dc, piece):
        cc = (c + dc) % C
        return remote(
            out_part.at[piece, cc],
            out_ref.at[c, :, :, pl.ds(piece * R, R)],
            o_send.at[dc, piece],
            o_recv.at[dc, piece],
            device(x, cc, b),
        )

    for piece in range(X):
        for head in range(KVL):
            mixed = acc_ref[piece, head] / sum_ref[piece, head]
            out_part[piece, :, head] = mixed.astype(jnp.bfloat16).reshape(C, G, R, D)
        for dc in range(1, C):
            o_copy(dc, piece).start()
        out_ref[c, :, :, pl.ds(piece * R, R)] = out_part[piece, c]

    for dx, dc in offsets:
        kv_copy(dx, dc).wait_send()
        q_copy(dx, dc).wait_send()
    for piece in range(X):
        small_loop(1, Z, lambda k: z_copy(k, piece).wait_send())

        def sent(k):
            small_loop(1, Y, lambda m: y_copy(k, m, piece).wait_send())

        small_loop(0, Z, sent)
    for piece in range(X):
        for dc in range(1, C):
            o_copy(dc, piece).wait()


def per_device(queries, keys, values, run_index):
    X, C, B = lax.axis_size("heads"), lax.axis_size("team"), lax.axis_size("blk")
    R, QH, D = queries.shape[1:]
    KVH = keys.shape[2]
    KVL = KVH // (X * C)
    G = QH // KVH
    Y = max(d for d in range(1, math.isqrt(B) + 1) if B % d == 0)
    Z = B // Y
    freqs = inverse_freqs(D)
    freqs = jnp.asarray(np.concatenate([freqs, freqs])[None], jnp.float32)
    rows = C * G * R
    vmem = pl.BlockSpec(memory_space=pltpu.VMEM)
    dma = pltpu.SemaphoreType.DMA
    bf16, f32 = jnp.bfloat16, jnp.float32
    out = pl.pallas_call(
        functools.partial(attend_kernel, (X, C, Z, Y, R, KVL, G, D)),
        out_shape=jax.ShapeDtypeStruct((C, KVL, G, X * R, D), bf16),
        in_specs=[pl.BlockSpec(memory_space=pltpu.SMEM)] + [vmem] * 4,
        out_specs=vmem,
        scratch_shapes=[
            pltpu.VMEM((X * C, 2, KVL, R, D), bf16),
            pltpu.VMEM((X * C, KVL, G, R, D), bf16),
            pltpu.VMEM((Z, Y, X, 2, KVL, C, R, D), bf16),
            pltpu.VMEM((X, KVL, C, G, R, D), bf16),
            pltpu.VMEM((X, KVL, rows, D), f32),
            pltpu.VMEM((X, KVL, rows, 1), f32),
            pltpu.VMEM((X, KVL, rows, 1), f32),
            pltpu.VMEM((X, C, KVL, G, R, D), bf16),
            dma((X, C)),
            dma((X, C)),
            dma((X, C)),
            dma((X, C)),
            dma((Z, X)),
            dma((Z, X)),
            dma((Z, Y, X)),
            dma((Z, Y, X)),
            dma((C, X)),
            dma((C, X)),
        ],
        compiler_params=pltpu.CompilerParams(
            collective_id=0, has_side_effects=True, vmem_limit_bytes=48 * 2**20
        ),
    )(run_index, freqs, queries, keys, values)
    return jnp.transpose(out.reshape(C * KVL * G, X * R, D), (1, 0, 2))


def solution(mesh):
    in_specs = (
        P("heads", ("team", "blk"), None, None),
        P("heads", ("team", "blk"), None, None),
        P("heads", ("team", "blk"), None, None),
        P(),
    )
    out_specs = P(("team", "blk"), "heads", None)
    return jax.shard_map(
        per_device, mesh=mesh, in_specs=in_specs, out_specs=out_specs, check_vma=False
    )
```

```python
import functools
import math

import jax
import jax.numpy as jnp
import numpy as np
from jax import lax
from jax.experimental import pallas as pl
from jax.experimental.pallas import tpu as pltpu
from jax.sharding import PartitionSpec as P

mask_floor = -1e30
rope_theta = 500000.0
rope_factor = 8.0
low_factor = 1.0
high_factor = 4.0
initial_context = 8192.0


def inverse_freqs(head_width):
    counter = np.arange(head_width // 2, dtype=np.float64)
    base_freq = 1.0 / rope_theta ** (2.0 * counter / head_width)
    wavelength = 2.0 * np.pi / base_freq
    smooth = (initial_context / wavelength - low_factor) / (high_factor - low_factor)
    blended = (1.0 - smooth) * base_freq / rope_factor + smooth * base_freq
    middle = np.where(wavelength > initial_context / low_factor, base_freq / rope_factor, blended)
    return np.where(wavelength < initial_context / high_factor, base_freq, middle)


def small_loop(first, last, body):
    if last - first <= 4:
        for at in range(first, last):
            body(at)
    else:
        lax.fori_loop(first, last, lambda at, unused: (body(at), unused)[1], 0)


def attend_kernel(
    dims,
    run_hbm,
    freq_hbm,
    q_hbm,
    k_hbm,
    v_hbm,
    out_ref,
    run_ref,
    freq_ref,
    q_ref,
    k_ref,
    v_ref,
    load_sem,
    kv_out,
    q_out,
    kv_all,
    q_all,
    acc_ref,
    max_ref,
    sum_ref,
    out_part,
    kv_send,
    kv_recv,
    q_send,
    q_recv,
    z_send,
    z_recv,
    y_send,
    y_recv,
    o_send,
    o_recv,
):
    X, C, Z, Y, R, KVL, G, D = dims
    S = C * Z * Y
    half = X * R // 2
    rows = C * G * R
    x, c, b = lax.axis_index("heads"), lax.axis_index("team"), lax.axis_index("blk")
    z, y = b // Y, b % Y
    mine = x * C + c
    def y_to(m):
        return (y + m) % Y

    def y_from(m):
        return (y + Y - m) % Y

    def device(xx, cc, bb):
        return {"heads": xx, "team": cc, "blk": bb}

    loads = [
        pltpu.make_async_copy(src, dst, load_sem.at[at])
        for at, (src, dst) in enumerate(
            [(run_hbm, run_ref), (freq_hbm, freq_ref), (k_hbm, k_ref), (v_hbm, v_ref), (q_hbm, q_ref)]
        )
    ]
    for load in loads:
        load.start()

    low, high = z, Z - 1 - z
    near = jnp.minimum(low, high)

    def z_near(k):
        if isinstance(k, int) and k == 0:
            return z
        paired = jnp.where(k % 2 == 1, z - (k + 1) // 2, z + k // 2)
        single = jnp.where(low < high, z + (k - near), z - (k - near))
        return jnp.where(k <= 2 * near, paired, single)

    offsets = [(dx, dc) for dx in range(X) for dc in range(C) if (dx, dc) != (0, 0)]

    barrier = pltpu.get_barrier_semaphore()

    def greet(xx, cc, bb):
        pl.semaphore_signal(
            barrier, inc=1, device_id=device(xx, cc, bb), device_id_type=pl.DeviceIdType.MESH
        )

    for dx, dc in offsets:
        greet((x + dx) % X, (c + dc) % C, b)
    pl.when(z > 0)(lambda: greet(x, c, b - Y))
    pl.when(z < Z - 1)(lambda: greet(x, c, b + Y))
    small_loop(1, Y, lambda m: greet(x, c, z * Y + y_to(m)))

    def first_pos(slot, piece):
        run = run_ref[slot]
        start = piece * R
        if isinstance(piece, int):
            return run * half + start if start < half else (2 * S - 1 - run) * half + start - half
        return jnp.where(start < half, run * half, (2 * S - 1 - run) * half - half) + start

    loads[0].wait()
    loads[1].wait()

    own_first = first_pos(c * (Z * Y) + b, x)
    pos = own_first + lax.broadcasted_iota(jnp.int32, (R, D), 0)
    angles = pos.astype(jnp.float32) * freq_ref[...]
    cosine = jnp.cos(angles)
    sine = jnp.sin(angles)
    lanes = lax.broadcasted_iota(jnp.int32, (R, D), 1)
    sine = jnp.where(lanes < D // 2, -sine, sine)

    def by_head(ref, first, count):
        return jnp.swapaxes(ref[0, :, first : first + count, :].astype(jnp.float32), 0, 1)

    def rotated(values):
        turned = pltpu.roll(values, D // 2, 2)
        return values * cosine[None] + turned * sine[None]

    loads[2].wait()
    loads[3].wait()
    kv_heads = X * C * KVL
    kv_out[:, 0] = (
        rotated(by_head(k_ref, 0, kv_heads)).astype(jnp.bfloat16).reshape(X * C, KVL, R, D)
    )
    kv_out[:, 1] = by_head(v_ref, 0, kv_heads).astype(jnp.bfloat16).reshape(X * C, KVL, R, D)
    kv_all[z, 0, x, :, :, c] = kv_out[mine]

    pl.semaphore_wait(barrier, len(offsets) + Y - 1 + jnp.minimum(z, 1) + jnp.minimum(Z - 1 - z, 1))

    def remote(src, dst, send, recv, to):
        return pltpu.make_async_remote_copy(
            src_ref=src,
            dst_ref=dst,
            send_sem=send,
            recv_sem=recv,
            device_id=to,
            device_id_type=pl.DeviceIdType.MESH,
        )

    def kv_copy(dx, dc):
        xx, cc = (x + dx) % X, (c + dc) % C
        return remote(
            kv_out.at[xx * C + cc],
            kv_all.at[z, 0, x, :, :, c],
            kv_send.at[dx, dc],
            kv_recv.at[dx, dc],
            device(xx, cc, b),
        )

    def q_copy(dx, dc):
        xx, cc = (x + dx) % X, (c + dc) % C
        return remote(
            q_out.at[xx * C + cc],
            q_all.at[x, :, c],
            q_send.at[dx, dc],
            q_recv.at[dx, dc],
            device(xx, cc, b),
        )

    for dx, dc in offsets:
        kv_copy(dx, dc).start()

    loads[4].wait()
    q_heads = KVL * G
    for to in range(X * C):
        q_out[to] = (
            rotated(by_head(q_ref, to * q_heads, q_heads))
            .astype(jnp.bfloat16)
            .reshape(KVL, G, R, D)
        )
    q_all[x, :, c] = q_out[mine]
    for dx, dc in offsets:
        q_copy(dx, dc).start()

    def z_copy(at, up, piece):
        return remote(
            kv_all.at[at, 0, piece],
            kv_all.at[at, 0, piece],
            z_send.at[up, at, piece],
            z_recv.at[at, piece],
            device(x, c, b + Y if up else b - Y),
        )

    def y_copy(at, m, piece):
        return remote(
            kv_all.at[at, 0, piece],
            kv_all.at[at, m, piece],
            y_send.at[at, m, piece],
            y_recv.at[at, m, piece],
            device(x, c, z * Y + y_to(m)),
        )

    def piece_at(dx):
        return (x + X - dx) % X

    def pass_on(at, piece):
        pl.when((at <= z) & (z < Z - 1))(lambda: z_copy(at, 1, piece).start())
        pl.when((at >= z) & (z > 0))(lambda: z_copy(at, 0, piece).start())
        small_loop(1, Y, lambda m: y_copy(at, m, piece).start())

    for dx in range(X):
        for dc in range(C):
            if (dx, dc) != (0, 0):
                kv_copy(dx, dc).wait_recv()
        pass_on(z, piece_at(dx))

    def receive(k):
        at = z_near(k)
        for dx in range(X):
            z_copy(at, 1, piece_at(dx)).wait_recv()
            pass_on(at, piece_at(dx))

    scaling = math.log2(math.e) * D ** (-0.5)

    def key_positions(k, pieces):
        count = len(pieces) * Y * C * R
        lane = lax.broadcasted_iota(jnp.int32, (1, count), 1)
        segment = lane // R
        total = lane % R
        at = 0
        for piece in pieces:
            for m in range(Y):
                for t in range(C):
                    slot = t * (Z * Y) + z_near(k) * Y + y_from(m)
                    total = total + jnp.where(segment == at, first_pos(slot, piece), 0)
                    at += 1
        return total

    def query_positions(piece):
        row = lax.broadcasted_iota(jnp.int32, (rows, 1), 0)
        total = row % R
        for t in range(C):
            total = total + jnp.where(row // (G * R) == t, first_pos(t * (Z * Y) + b, piece), 0)
        return total

    early = list(range(X // 2))
    late = list(range(X // 2, X))

    def attend(k, first):
        at = z_near(k)

        def units(kind, head, pieces):
            return jnp.concatenate(
                [kv_all[at, m, p, kind, head].reshape(C * R, D) for p in pieces for m in range(Y)],
                axis=0,
            )

        key_pos = {"early": key_positions(k, early), "late": key_positions(k, late)}
        for head in range(KVL):
            keys = {"early": units(0, head, early), "late": units(0, head, late)}
            values = {"early": units(1, head, early), "late": units(1, head, late)}
            for piece in range(X):
                query = q_all[piece, head].reshape(rows, D)
                query_pos = query_positions(piece)
                own = "early" if piece in early else "late"
                parts = ["early"] if own == "early" else ["early", "late"]
                scores = []
                for part in parts:
                    s = lax.dot_general(
                        query, keys[part], (((1,), (1,)), ((), ())),
                        preferred_element_type=jnp.float32,
                    )
                    if part == own:
                        s = jnp.where(key_pos[part] <= query_pos, s, mask_floor)
                    scores.append(s)
                top = functools.reduce(
                    jnp.maximum, [jnp.max(s, axis=-1, keepdims=True) for s in scores]
                )
                if not first:
                    before = max_ref[piece, head]
                    top = jnp.maximum(top, before)
                    factor = jnp.exp2((before - top) * scaling)
                weights = [jnp.exp2((s - top) * scaling) for s in scores]
                total = sum(jnp.sum(w, axis=-1, keepdims=True) for w in weights)
                update = sum(
                    jnp.dot(
                        w.astype(jnp.bfloat16), values[part], preferred_element_type=jnp.float32
                    )
                    for w, part in zip(weights, parts)
                )
                if not first:
                    total = total + sum_ref[piece, head] * factor
                    update = update + acc_ref[piece, head] * factor
                max_ref[piece, head] = top
                sum_ref[piece, head] = total
                acc_ref[piece, head] = update


    if Z > 1:
        receive(1)
    for dx, dc in offsets:
        q_copy(dx, dc).wait_recv()

    def arrive(k):
        for dx in range(X):
            piece = piece_at(dx)
            small_loop(1, Y, lambda m: y_copy(z_near(k), m, piece).wait_recv())

    arrive(0)
    attend(0, True)

    def later(k):
        if isinstance(k, int):
            if k + 1 < Z:
                receive(k + 1)
        else:
            pl.when(k + 1 < Z)(lambda: receive(k + 1))
        arrive(k)
        attend(k, False)

    small_loop(1, Z, later)

    def o_copy(dc, piece):
        cc = (c + dc) % C
        return remote(
            out_part.at[piece, cc],
            out_ref.at[c, :, :, pl.ds(piece * R, R)],
            o_send.at[dc, piece],
            o_recv.at[dc, piece],
            device(x, cc, b),
        )

    def own_copy(piece):
        return pltpu.make_async_copy(
            out_part.at[piece, c], out_ref.at[c, :, :, pl.ds(piece * R, R)], o_send.at[0, piece]
        )

    for piece in range(X):
        for head in range(KVL):
            mixed = acc_ref[piece, head] / sum_ref[piece, head]
            out_part[piece, :, head] = mixed.astype(jnp.bfloat16).reshape(C, G, R, D)
        for dc in range(1, C):
            o_copy(dc, piece).start()
        own_copy(piece).start()

    for dx, dc in offsets:
        kv_copy(dx, dc).wait_send()
        q_copy(dx, dc).wait_send()
    for piece in range(X):

        def sent(at):
            pl.when((at <= z) & (z < Z - 1))(lambda: z_copy(at, 1, piece).wait_send())
            pl.when((at >= z) & (z > 0))(lambda: z_copy(at, 0, piece).wait_send())
            small_loop(1, Y, lambda m: y_copy(at, m, piece).wait_send())

        small_loop(0, Z, sent)
    for piece in range(X):
        for dc in range(1, C):
            o_copy(dc, piece).wait()
        own_copy(piece).wait()


def per_device(queries, keys, values, run_index):
    X, C, B = lax.axis_size("heads"), lax.axis_size("team"), lax.axis_size("blk")
    R, QH, D = queries.shape[1:]
    KVH = keys.shape[2]
    KVL = KVH // (X * C)
    G = QH // KVH
    Y = max(d for d in range(1, math.isqrt(B) + 1) if B % d == 0)
    Z = B // Y
    freqs = inverse_freqs(D)
    freqs = jnp.asarray(np.concatenate([freqs, freqs])[None], jnp.float32)
    rows = C * G * R
    hbm = pl.BlockSpec(memory_space=pltpu.HBM)
    dma = pltpu.SemaphoreType.DMA
    bf16, f32 = jnp.bfloat16, jnp.float32
    out = pl.pallas_call(
        functools.partial(attend_kernel, (X, C, Z, Y, R, KVL, G, D)),
        out_shape=jax.ShapeDtypeStruct((C, KVL, G, X * R, D), bf16),
        in_specs=[hbm] * 5,
        out_specs=hbm,
        scratch_shapes=[
            pltpu.SMEM(run_index.shape, run_index.dtype),
            pltpu.VMEM(freqs.shape, f32),
            pltpu.VMEM(queries.shape, bf16),
            pltpu.VMEM(keys.shape, bf16),
            pltpu.VMEM(values.shape, bf16),
            dma((5,)),
            pltpu.VMEM((X * C, 2, KVL, R, D), bf16),
            pltpu.VMEM((X * C, KVL, G, R, D), bf16),
            pltpu.VMEM((Z, Y, X, 2, KVL, C, R, D), bf16),
            pltpu.VMEM((X, KVL, C, G, R, D), bf16),
            pltpu.VMEM((X, KVL, rows, D), f32),
            pltpu.VMEM((X, KVL, rows, 1), f32),
            pltpu.VMEM((X, KVL, rows, 1), f32),
            pltpu.VMEM((X, C, KVL, G, R, D), bf16),
            dma((X, C)),
            dma((X, C)),
            dma((X, C)),
            dma((X, C)),
            dma((2, Z, X)),
            dma((Z, X)),
            dma((Z, Y, X)),
            dma((Z, Y, X)),
            dma((C, X)),
            dma((C, X)),
        ],
        compiler_params=pltpu.CompilerParams(
            collective_id=0, has_side_effects=True, vmem_limit_bytes=64 * 2**20
        ),
    )(run_index, freqs, queries, keys, values)
    return jnp.transpose(out.reshape(C * KVL * G, X * R, D), (1, 0, 2))


def solution(mesh):
    in_specs = (
        P("heads", ("team", "blk"), None, None),
        P("heads", ("team", "blk"), None, None),
        P("heads", ("team", "blk"), None, None),
        P(),
    )
    out_specs = P(("team", "blk"), "heads", None)
    return jax.shard_map(
        per_device, mesh=mesh, in_specs=in_specs, out_specs=out_specs, check_vma=False
    )
```

```python
import functools
import math

import jax
import jax.numpy as jnp
import numpy as np
from jax import lax
from jax.experimental import pallas as pl
from jax.experimental.pallas import tpu as pltpu
from jax.sharding import PartitionSpec as P

mask_floor = -1e30
rope_theta = 500000.0
rope_factor = 8.0
low_factor = 1.0
high_factor = 4.0
initial_context = 8192.0


def inverse_freqs(head_width):
    counter = np.arange(head_width // 2, dtype=np.float64)
    base_freq = 1.0 / rope_theta ** (2.0 * counter / head_width)
    wavelength = 2.0 * np.pi / base_freq
    smooth = (initial_context / wavelength - low_factor) / (high_factor - low_factor)
    blended = (1.0 - smooth) * base_freq / rope_factor + smooth * base_freq
    middle = np.where(wavelength > initial_context / low_factor, base_freq / rope_factor, blended)
    return np.where(wavelength < initial_context / high_factor, base_freq, middle)


def small_loop(first, last, body):
    if last - first <= 4:
        for at in range(first, last):
            body(at)
    else:
        lax.fori_loop(first, last, lambda at, unused: (body(at), unused)[1], 0)


def attend_kernel(
    dims,
    run_hbm,
    freq_hbm,
    q_hbm,
    k_hbm,
    v_hbm,
    out_ref,
    run_ref,
    freq_ref,
    q_ref,
    k_ref,
    v_ref,
    load_sem,
    kv_out,
    q_out,
    kv_all,
    q_all,
    acc_ref,
    max_ref,
    sum_ref,
    pos_ref,
    out_part,
    kv_send,
    kv_recv,
    q_send,
    q_recv,
    z_send,
    z_recv,
    y_send,
    y_recv,
    o_send,
    o_recv,
):
    X, C, Z, Y, R, KVL, G, D = dims
    S = C * Z * Y
    half = X * R // 2
    rows = C * G * R
    x, c, b = lax.axis_index("heads"), lax.axis_index("team"), lax.axis_index("blk")
    z, y = b // Y, b % Y
    mine = x * C + c
    def y_to(m):
        return (y + m) % Y

    def y_from(m):
        return (y + Y - m) % Y

    def device(xx, cc, bb):
        return {"heads": xx, "team": cc, "blk": bb}

    loads = [
        pltpu.make_async_copy(src, dst, load_sem.at[at])
        for at, (src, dst) in enumerate(
            [(run_hbm, run_ref), (freq_hbm, freq_ref), (k_hbm, k_ref), (v_hbm, v_ref), (q_hbm, q_ref)]
        )
    ]
    for load in loads:
        load.start()

    low, high = z, Z - 1 - z
    near = jnp.minimum(low, high)

    def z_near(k):
        if isinstance(k, int) and k == 0:
            return z
        paired = jnp.where(k % 2 == 1, z - (k + 1) // 2, z + k // 2)
        single = jnp.where(low < high, z + (k - near), z - (k - near))
        return jnp.where(k <= 2 * near, paired, single)

    offsets = [(dx, dc) for dx in range(X) for dc in range(C) if (dx, dc) != (0, 0)]

    barrier = pltpu.get_barrier_semaphore()

    def greet(xx, cc, bb):
        pl.semaphore_signal(
            barrier, inc=1, device_id=device(xx, cc, bb), device_id_type=pl.DeviceIdType.MESH
        )

    for dx, dc in offsets:
        greet((x + dx) % X, (c + dc) % C, b)
    pl.when(z > 0)(lambda: greet(x, c, b - Y))
    pl.when(z < Z - 1)(lambda: greet(x, c, b + Y))
    small_loop(1, Y, lambda m: greet(x, c, z * Y + y_to(m)))

    def first_pos(slot, piece):
        run = run_ref[slot]
        start = piece * R
        if isinstance(piece, int):
            return run * half + start if start < half else (2 * S - 1 - run) * half + start - half
        return jnp.where(start < half, run * half, (2 * S - 1 - run) * half - half) + start

    loads[0].wait()
    loads[1].wait()

    own_first = first_pos(c * (Z * Y) + b, x)
    pos = own_first + lax.broadcasted_iota(jnp.int32, (R, D), 0)
    angles = pos.astype(jnp.float32) * freq_ref[...]
    cosine = jnp.cos(angles)
    sine = jnp.sin(angles)
    lanes = lax.broadcasted_iota(jnp.int32, (R, D), 1)
    sine = jnp.where(lanes < D // 2, -sine, sine)

    def by_head(ref, first, count):
        return jnp.swapaxes(ref[0, :, first : first + count, :].astype(jnp.float32), 0, 1)

    def rotated(values):
        turned = pltpu.roll(values, D // 2, 2)
        return values * cosine[None] + turned * sine[None]

    loads[2].wait()
    loads[3].wait()
    kv_heads = X * C * KVL
    kv_out[:, 0] = (
        rotated(by_head(k_ref, 0, kv_heads)).astype(jnp.bfloat16).reshape(X * C, KVL, R, D)
    )
    kv_out[:, 1] = by_head(v_ref, 0, kv_heads).astype(jnp.bfloat16).reshape(X * C, KVL, R, D)
    kv_all[z, 0, x, c] = kv_out[mine]

    pl.semaphore_wait(barrier, len(offsets) + Y - 1 + jnp.minimum(z, 1) + jnp.minimum(Z - 1 - z, 1))

    def remote(src, dst, send, recv, to):
        return pltpu.make_async_remote_copy(
            src_ref=src,
            dst_ref=dst,
            send_sem=send,
            recv_sem=recv,
            device_id=to,
            device_id_type=pl.DeviceIdType.MESH,
        )

    units_here = [
        ((x + X - dx) % X, (c + C - dc) % C) for dx in range(X) for dc in range(C)
    ]

    def z_copy(at, up, unit):
        return remote(
            kv_all.at[at, 0, *unit],
            kv_all.at[at, 0, *unit],
            z_send.at[up, at, *unit],
            z_recv.at[at, *unit],
            device(x, c, b + Y if up else b - Y),
        )

    def y_copy(at, m, unit):
        return remote(
            kv_all.at[at, 0, *unit],
            kv_all.at[at, m, *unit],
            y_send.at[at, m, *unit],
            y_recv.at[at, m, *unit],
            device(x, c, z * Y + y_to(m)),
        )

    def pass_on(at, unit):
        pl.when((at <= z) & (z < Z - 1))(lambda: z_copy(at, 1, unit).start())
        pl.when((at >= z) & (z > 0))(lambda: z_copy(at, 0, unit).start())
        small_loop(1, Y, lambda m: y_copy(at, m, unit).start())

    def kv_copy(dx, dc):
        xx, cc = (x + dx) % X, (c + dc) % C
        return remote(
            kv_out.at[xx * C + cc],
            kv_all.at[z, 0, x, c],
            kv_send.at[dx, dc],
            kv_recv.at[dx, dc],
            device(xx, cc, b),
        )

    def q_copy(dx, dc):
        xx, cc = (x + dx) % X, (c + dc) % C
        return remote(
            q_out.at[xx * C + cc],
            q_all.at[x, :, c],
            q_send.at[dx, dc],
            q_recv.at[dx, dc],
            device(xx, cc, b),
        )

    for dx, dc in offsets:
        kv_copy(dx, dc).start()
    pass_on(z, units_here[0])

    loads[4].wait()
    q_heads = KVL * G
    for to in range(X * C):
        q_out[to] = (
            rotated(by_head(q_ref, to * q_heads, q_heads))
            .astype(jnp.bfloat16)
            .reshape(KVL, G, R, D)
        )
    q_all[x, :, c] = q_out[mine]
    for dx, dc in offsets:
        q_copy(dx, dc).start()
    for (dx, dc), unit in zip(offsets, units_here[1:]):
        kv_copy(dx, dc).wait_recv()
        pass_on(z, unit)

    def receive(k):
        at = z_near(k)
        for unit in units_here:
            z_copy(at, 1, unit).wait_recv()
            pass_on(at, unit)

    scaling = math.log2(math.e) * D ** (-0.5)

    def key_positions(k, pieces):
        count = len(pieces) * Y * C * R
        lane = lax.broadcasted_iota(jnp.int32, (1, count), 1)
        segment = lane // R
        total = lane % R
        at = 0
        for piece in pieces:
            for m in range(Y):
                for t in range(C):
                    slot = t * (Z * Y) + z_near(k) * Y + y_from(m)
                    total = total + jnp.where(segment == at, first_pos(slot, piece), 0)
                    at += 1
        return total

    def query_positions(piece):
        row = lax.broadcasted_iota(jnp.int32, (rows, D), 0)
        total = row % R
        for t in range(C):
            total = total + jnp.where(row // (G * R) == t, first_pos(t * (Z * Y) + b, piece), 0)
        return total

    for piece in range(X):
        pos_ref[piece] = query_positions(piece)

    early = list(range(X // 2))
    late = list(range(X // 2, X))

    def attend(k, first):
        at = z_near(k)

        def units(kind, head, pieces):
            return jnp.concatenate(
                [
                    kv_all[at, m, p, t, kind, head]
                    for p in pieces
                    for m in range(Y)
                    for t in range(C)
                ],
                axis=0,
            )

        key_pos = {"early": key_positions(k, early), "late": key_positions(k, late)}
        for head in range(KVL):
            keys = {"early": units(0, head, early), "late": units(0, head, late)}
            values = {"early": units(1, head, early), "late": units(1, head, late)}
            for piece in range(X):
                query = q_all[piece, head].reshape(rows, D)
                own = "early" if piece in early else "late"
                parts = ["early"] if own == "early" else ["early", "late"]
                scores = []
                for part in parts:
                    s = lax.dot_general(
                        query, keys[part], (((1,), (1,)), ((), ())),
                        preferred_element_type=jnp.float32,
                    )
                    for start in range(0, s.shape[1], D):
                        column = s[:, start : start + D]
                        if part == own:
                            seen = key_pos[part][:, start : start + D] <= pos_ref[piece]
                            column = jnp.where(seen, column, mask_floor)
                        scores.append(column)
                top = jnp.max(functools.reduce(jnp.maximum, scores), axis=-1, keepdims=True)
                top = jnp.broadcast_to(top, (rows, D))
                if not first:
                    before = max_ref[piece, head]
                    top = jnp.maximum(top, before)
                    factor = jnp.exp2((before - top) * scaling)
                weights = [jnp.exp2((s - top) * scaling) for s in scores]
                total = sum(weights)
                update = jnp.dot(
                    jnp.concatenate([w.astype(jnp.bfloat16) for w in weights], axis=1),
                    jnp.concatenate([values[part] for part in parts], axis=0),
                    preferred_element_type=jnp.float32,
                )
                if not first:
                    total = total + sum_ref[piece, head] * factor
                    update = update + acc_ref[piece, head] * factor
                max_ref[piece, head] = top
                sum_ref[piece, head] = total
                acc_ref[piece, head] = update


    if Z > 1:
        receive(1)
    for dx, dc in offsets:
        q_copy(dx, dc).wait_recv()

    def arrive(k):
        for unit in units_here:
            small_loop(1, Y, lambda m: y_copy(z_near(k), m, unit).wait_recv())

    arrive(0)
    attend(0, True)

    def later(k):
        if isinstance(k, int):
            if k + 1 < Z:
                receive(k + 1)
        else:
            pl.when(k + 1 < Z)(lambda: receive(k + 1))
        arrive(k)
        attend(k, False)

    small_loop(1, Z, later)

    def o_copy(dc, piece):
        cc = (c + dc) % C
        return remote(
            out_part.at[piece, cc],
            out_ref.at[c, :, :, pl.ds(piece * R, R)],
            o_send.at[dc, piece],
            o_recv.at[dc, piece],
            device(x, cc, b),
        )

    for piece in range(X):
        for head in range(KVL):
            mixed = acc_ref[piece, head] / jnp.sum(sum_ref[piece, head], axis=-1, keepdims=True)
            out_part[piece, :, head] = mixed.astype(jnp.bfloat16).reshape(C, G, R, D)
        for dc in range(1, C):
            o_copy(dc, piece).start()
        out_ref[c, :, :, pl.ds(piece * R, R)] = out_part[piece, c]

    for dx, dc in offsets:
        kv_copy(dx, dc).wait_send()
        q_copy(dx, dc).wait_send()
    for unit in units_here:

        def sent(at):
            pl.when((at <= z) & (z < Z - 1))(lambda: z_copy(at, 1, unit).wait_send())
            pl.when((at >= z) & (z > 0))(lambda: z_copy(at, 0, unit).wait_send())
            small_loop(1, Y, lambda m: y_copy(at, m, unit).wait_send())

        small_loop(0, Z, sent)
    for piece in range(X):
        for dc in range(1, C):
            o_copy(dc, piece).wait()


def per_device(queries, keys, values, run_index):
    X, C, B = lax.axis_size("heads"), lax.axis_size("team"), lax.axis_size("blk")
    R, QH, D = queries.shape[1:]
    KVH = keys.shape[2]
    KVL = KVH // (X * C)
    G = QH // KVH
    Y = max(d for d in range(1, math.isqrt(B) + 1) if B % d == 0)
    Z = B // Y
    freqs = inverse_freqs(D)
    freqs = jnp.asarray(np.concatenate([freqs, freqs])[None], jnp.float32)
    rows = C * G * R
    hbm = pl.BlockSpec(memory_space=pltpu.HBM)
    dma = pltpu.SemaphoreType.DMA
    bf16, f32 = jnp.bfloat16, jnp.float32
    out = pl.pallas_call(
        functools.partial(attend_kernel, (X, C, Z, Y, R, KVL, G, D)),
        out_shape=pltpu.VMEM((C, KVL, G, X * R, D), bf16),
        in_specs=[hbm] * 5,
        out_specs=pl.BlockSpec(memory_space=pltpu.VMEM),
        scratch_shapes=[
            pltpu.SMEM(run_index.shape, run_index.dtype),
            pltpu.VMEM(freqs.shape, f32),
            pltpu.VMEM(queries.shape, bf16),
            pltpu.VMEM(keys.shape, bf16),
            pltpu.VMEM(values.shape, bf16),
            dma((5,)),
            pltpu.VMEM((X * C, 2, KVL, R, D), bf16),
            pltpu.VMEM((X * C, KVL, G, R, D), bf16),
            pltpu.VMEM((Z, Y, X, C, 2, KVL, R, D), bf16),
            pltpu.VMEM((X, KVL, C, G, R, D), bf16),
            pltpu.VMEM((X, KVL, rows, D), f32),
            pltpu.VMEM((X, KVL, rows, D), f32),
            pltpu.VMEM((X, KVL, rows, D), f32),
            pltpu.VMEM((X, rows, D), jnp.int32),
            pltpu.VMEM((X, C, KVL, G, R, D), bf16),
            dma((X, C)),
            dma((X, C)),
            dma((X, C)),
            dma((X, C)),
            dma((2, Z, X, C)),
            dma((Z, X, C)),
            dma((Z, Y, X, C)),
            dma((Z, Y, X, C)),
            dma((C, X)),
            dma((C, X)),
        ],
        compiler_params=pltpu.CompilerParams(
            collective_id=0, has_side_effects=True, vmem_limit_bytes=60 * 2**20
        ),
    )(run_index, freqs, queries, keys, values)
    return jnp.transpose(out.reshape(C * KVL * G, X * R, D), (1, 0, 2))


def solution(mesh):
    in_specs = (
        P("heads", ("team", "blk"), None, None),
        P("heads", ("team", "blk"), None, None),
        P("heads", ("team", "blk"), None, None),
        P(),
    )
    out_specs = P(("team", "blk"), "heads", None)
    return jax.shard_map(
        per_device, mesh=mesh, in_specs=in_specs, out_specs=out_specs, check_vma=False
    )
```

```python
import functools
import math

import jax
import jax.numpy as jnp
import numpy as np
from jax import lax
from jax.experimental import pallas as pl
from jax.experimental.pallas import tpu as pltpu
from jax.sharding import PartitionSpec as P

mask_floor = -1e30
rope_theta = 500000.0
rope_factor = 8.0
low_factor = 1.0
high_factor = 4.0
initial_context = 8192.0


def inverse_freqs(head_width):
    counter = np.arange(head_width // 2, dtype=np.float64)
    base_freq = 1.0 / rope_theta ** (2.0 * counter / head_width)
    wavelength = 2.0 * np.pi / base_freq
    smooth = (initial_context / wavelength - low_factor) / (high_factor - low_factor)
    blended = (1.0 - smooth) * base_freq / rope_factor + smooth * base_freq
    middle = np.where(wavelength > initial_context / low_factor, base_freq / rope_factor, blended)
    return np.where(wavelength < initial_context / high_factor, base_freq, middle)


def small_loop(first, last, body):
    if last - first <= 4:
        for at in range(first, last):
            body(at)
    else:
        lax.fori_loop(first, last, lambda at, unused: (body(at), unused)[1], 0)


def attend_kernel(
    dims,
    run_hbm,
    freq_hbm,
    q_hbm,
    k_hbm,
    v_hbm,
    out_ref,
    run_ref,
    freq_ref,
    q_ref,
    k_ref,
    v_ref,
    load_sem,
    kv_out,
    q_out,
    kv_all,
    q_all,
    acc_ref,
    max_ref,
    sum_ref,
    pos_ref,
    out_part,
    kv_send,
    kv_recv,
    q_send,
    q_recv,
    z_send,
    z_recv,
    o_send,
    o_recv,
):
    X, C, Z, Y, R, KVL, G, D = dims
    S = C * Z * Y
    half = X * R // 2
    rows = C * G * R
    x, c, b = lax.axis_index("heads"), lax.axis_index("team"), lax.axis_index("blk")
    z, y = b // Y, b % Y
    mine = (x * Y + y) * C + c
    def device(xx, cc, bb):
        return {"heads": xx, "team": cc, "blk": bb}

    loads = [
        pltpu.make_async_copy(src, dst, load_sem.at[at])
        for at, (src, dst) in enumerate(
            [(run_hbm, run_ref), (freq_hbm, freq_ref), (k_hbm, k_ref), (v_hbm, v_ref), (q_hbm, q_ref)]
        )
    ]
    for load in loads:
        load.start()

    low, high = z, Z - 1 - z
    near = jnp.minimum(low, high)

    def z_near(k):
        if isinstance(k, int) and k == 0:
            return z
        paired = jnp.where(k % 2 == 1, z - (k + 1) // 2, z + k // 2)
        single = jnp.where(low < high, z + (k - near), z - (k - near))
        return jnp.where(k <= 2 * near, paired, single)

    offsets = [
        (dx, dy, dc)
        for dx in range(X)
        for dy in range(Y)
        for dc in range(C)
        if (dx, dy, dc) != (0, 0, 0)
    ]

    barrier = pltpu.get_barrier_semaphore()

    def greet(xx, cc, bb):
        pl.semaphore_signal(
            barrier, inc=1, device_id=device(xx, cc, bb), device_id_type=pl.DeviceIdType.MESH
        )

    def member(dx, dy, dc):
        return (x + dx) % X, (y + dy) % Y, (c + dc) % C

    for offset in offsets:
        xx, yy, cc = member(*offset)
        greet(xx, cc, z * Y + yy)
    pl.when(z > 0)(lambda: greet(x, c, b - Y))
    pl.when(z < Z - 1)(lambda: greet(x, c, b + Y))

    def first_pos(slot, piece):
        run = run_ref[slot]
        start = piece * R
        if isinstance(piece, int):
            return run * half + start if start < half else (2 * S - 1 - run) * half + start - half
        return jnp.where(start < half, run * half, (2 * S - 1 - run) * half - half) + start

    loads[0].wait()
    loads[1].wait()

    own_first = first_pos(c * (Z * Y) + b, x)
    pos = own_first + lax.broadcasted_iota(jnp.int32, (R, D), 0)
    angles = pos.astype(jnp.float32) * freq_ref[...]
    cosine = jnp.cos(angles)
    sine = jnp.sin(angles)
    lanes = lax.broadcasted_iota(jnp.int32, (R, D), 1)
    sine = jnp.where(lanes < D // 2, -sine, sine)

    def by_head(ref, first, count):
        return jnp.swapaxes(ref[0, :, first : first + count, :].astype(jnp.float32), 0, 1)

    def rotated(values):
        turned = pltpu.roll(values, D // 2, 2)
        return values * cosine[None] + turned * sine[None]

    loads[2].wait()
    loads[3].wait()
    kv_heads = X * Y * C * KVL
    kv_out[:, 0] = (
        rotated(by_head(k_ref, 0, kv_heads)).astype(jnp.bfloat16).reshape(X * Y * C, KVL, R, D)
    )
    kv_out[:, 1] = by_head(v_ref, 0, kv_heads).astype(jnp.bfloat16).reshape(X * Y * C, KVL, R, D)
    kv_all[z, x, y, c] = kv_out[mine]

    pl.semaphore_wait(barrier, len(offsets) + jnp.minimum(z, 1) + jnp.minimum(Z - 1 - z, 1))

    def remote(src, dst, send, recv, to):
        return pltpu.make_async_remote_copy(
            src_ref=src,
            dst_ref=dst,
            send_sem=send,
            recv_sem=recv,
            device_id=to,
            device_id_type=pl.DeviceIdType.MESH,
        )

    units_here = [((x + X - dx) % X, (y + Y - dy) % Y) for dx in range(X) for dy in range(Y)]

    def z_copy(at, up, unit):
        return remote(
            kv_all.at[at, *unit],
            kv_all.at[at, *unit],
            z_send.at[up, at, *unit],
            z_recv.at[at, *unit],
            device(x, c, b + Y if up else b - Y),
        )

    def pass_on(at, unit):
        pl.when((at <= z) & (z < Z - 1))(lambda: z_copy(at, 1, unit).start())
        pl.when((at >= z) & (z > 0))(lambda: z_copy(at, 0, unit).start())

    def kv_copy(*offset):
        xx, yy, cc = member(*offset)
        return remote(
            kv_out.at[(xx * Y + yy) * C + cc],
            kv_all.at[z, x, y, c],
            kv_send.at[*offset],
            kv_recv.at[*offset],
            device(xx, cc, z * Y + yy),
        )

    def q_copy(*offset):
        xx, yy, cc = member(*offset)
        return remote(
            q_out.at[(xx * Y + yy) * C + cc],
            q_all.at[x, :, y, c],
            q_send.at[*offset],
            q_recv.at[*offset],
            device(xx, cc, z * Y + yy),
        )

    for offset in offsets:
        kv_copy(*offset).start()

    loads[4].wait()
    q_heads = KVL * G
    for to in range(X * Y * C):
        q_out[to] = (
            rotated(by_head(q_ref, to * q_heads, q_heads))
            .astype(jnp.bfloat16)
            .reshape(KVL, G, R, D)
        )
    q_all[x, :, y, c] = q_out[mine]
    for offset in offsets:
        q_copy(*offset).start()
    for dx in range(X):
        for dy in range(Y):
            for dc in range(C):
                if (dx, dy, dc) != (0, 0, 0):
                    kv_copy(dx, dy, dc).wait_recv()
            pass_on(z, units_here[dx * Y + dy])

    def receive(k):
        at = z_near(k)
        for unit in units_here:
            z_copy(at, 1, unit).wait_recv()
            pass_on(at, unit)

    scaling = math.log2(math.e) * D ** (-0.5)

    def key_positions(k, pieces):
        count = len(pieces) * Y * C * R
        lane = lax.broadcasted_iota(jnp.int32, (1, count), 1)
        segment = lane // R
        total = lane % R
        at = 0
        for piece in pieces:
            for yy in range(Y):
                for cc in range(C):
                    slot = cc * (Z * Y) + z_near(k) * Y + yy
                    total = total + jnp.where(segment == at, first_pos(slot, piece), 0)
                    at += 1
        return total

    def query_positions(piece, yy):
        row = lax.broadcasted_iota(jnp.int32, (rows, D), 0)
        total = row % R
        for cc in range(C):
            slot = cc * (Z * Y) + z * Y + yy
            total = total + jnp.where(row // (G * R) == cc, first_pos(slot, piece), 0)
        return total

    for piece in range(X):
        for yy in range(Y):
            pos_ref[piece, yy] = query_positions(piece, yy)

    early = list(range(X // 2))
    late = list(range(X // 2, X))

    def attend(k, first, last):
        at = z_near(k)

        def units(kind, head, pieces):
            return jnp.concatenate(
                [
                    kv_all[at, p, yy, cc, kind, head]
                    for p in pieces
                    for yy in range(Y)
                    for cc in range(C)
                ],
                axis=0,
            )

        key_pos = {"early": key_positions(k, early), "late": key_positions(k, late)}
        for piece in range(X):
            own = "early" if piece in early else "late"
            parts = ["early"] if own == "early" else ["early", "late"]
            for dy in reversed(range(Y)):
                yy = (y + dy) % Y
                for head in range(KVL):
                    query = q_all[piece, head, yy].reshape(rows, D)
                    scores = []
                    for part in parts:
                        s = lax.dot_general(
                            query,
                            units(0, head, early if part == "early" else late),
                            (((1,), (1,)), ((), ())),
                            preferred_element_type=jnp.float32,
                        )
                        width = math.gcd(s.shape[1], D)
                        for start in range(0, s.shape[1], width):
                            column = s[:, start : start + width]
                            if part == own:
                                seen_to = pos_ref[piece, yy, :, :width]
                                seen = key_pos[part][:, start : start + width] <= seen_to
                                column = jnp.where(seen, column, mask_floor)
                            scores.append(column)
                    top = jnp.max(functools.reduce(jnp.maximum, scores), axis=-1, keepdims=True)
                    top = jnp.broadcast_to(top, (rows, D))
                    if not first:
                        before = max_ref[piece, head, yy]
                        top = jnp.maximum(top, before)
                        factor = jnp.exp2((before - top) * scaling)
                    weights = [jnp.exp2((s - top[:, :width]) * scaling) for s in scores]
                    total = sum(weights)
                    shared = units(1, head, early if own == "early" else early + late)
                    if width == D:
                        weights = [jnp.concatenate([w.astype(jnp.bfloat16) for w in weights], axis=1)]
                    else:
                        total = jnp.concatenate([total, jnp.zeros((rows, D - width), total.dtype)], axis=1)
                    update, start = 0.0, 0
                    for w in weights:
                        update = update + jnp.dot(
                            w.astype(jnp.bfloat16),
                            shared[start : start + w.shape[1]],
                            preferred_element_type=jnp.float32,
                        )
                        start += w.shape[1]
                    if not first:
                        total = total + sum_ref[piece, head, yy] * factor
                        update = update + acc_ref[piece, head, yy] * factor
                    if last:
                        mixed = update / jnp.sum(total, axis=-1, keepdims=True)
                        out_part[piece, yy, :, head] = mixed.astype(jnp.bfloat16).reshape(
                            C, G, R, D
                        )
                    else:
                        max_ref[piece, head, yy] = top
                        sum_ref[piece, head, yy] = total
                        acc_ref[piece, head, yy] = update
                if last:
                    for dc in reversed(range(C)):
                        if (dy, dc) != (0, 0):
                            o_copy(dy, dc, piece).start()
                        else:
                            out_ref[y * C + c, :, :, pl.ds(piece * R, R)] = out_part[piece, y, c]

    def o_copy(dy, dc, piece):
        xx, yy, cc = member(0, dy, dc)
        return remote(
            out_part.at[piece, yy, cc],
            out_ref.at[y * C + c, :, :, pl.ds(piece * R, R)],
            o_send.at[dy, dc, piece],
            o_recv.at[dy, dc, piece],
            device(x, cc, z * Y + yy),
        )

    if Z > 1:
        receive(1)
    for offset in offsets:
        q_copy(*offset).wait_recv()
    attend(0, True, Z == 1)

    def later(k):
        receive(k + 1)
        attend(k, False, False)

    small_loop(1, Z - 1, later)
    if Z > 1:
        attend(Z - 1, False, True)

    for offset in offsets:
        kv_copy(*offset).wait_send()
        q_copy(*offset).wait_send()
    for unit in units_here:

        def sent(at):
            pl.when((at <= z) & (z < Z - 1))(lambda: z_copy(at, 1, unit).wait_send())
            pl.when((at >= z) & (z > 0))(lambda: z_copy(at, 0, unit).wait_send())

        small_loop(0, Z, sent)
    for dx, dy, dc in offsets:
        if dx == 0:
            for piece in range(X):
                o_copy(dy, dc, piece).wait()


def per_device(queries, keys, values, run_index):
    X, C, B = lax.axis_size("heads"), lax.axis_size("team"), lax.axis_size("blk")
    R, QH, D = queries.shape[1:]
    KVH = keys.shape[2]
    Y = math.gcd(KVH // (X * C), B)
    KVL = KVH // (X * C * Y)
    G = QH // KVH
    Z = B // Y
    freqs = inverse_freqs(D)
    freqs = jnp.asarray(np.concatenate([freqs, freqs])[None], jnp.float32)
    rows = C * G * R
    hbm = pl.BlockSpec(memory_space=pltpu.HBM)
    dma = pltpu.SemaphoreType.DMA
    bf16, f32 = jnp.bfloat16, jnp.float32
    out = pl.pallas_call(
        functools.partial(attend_kernel, (X, C, Z, Y, R, KVL, G, D)),
        out_shape=pltpu.VMEM((Y * C, KVL, G, X * R, D), bf16),
        in_specs=[hbm] * 5,
        out_specs=pl.BlockSpec(memory_space=pltpu.VMEM),
        scratch_shapes=[
            pltpu.SMEM(run_index.shape, run_index.dtype),
            pltpu.VMEM(freqs.shape, f32),
            pltpu.VMEM(queries.shape, bf16),
            pltpu.VMEM(keys.shape, bf16),
            pltpu.VMEM(values.shape, bf16),
            dma((5,)),
            pltpu.VMEM((X * Y * C, 2, KVL, R, D), bf16),
            pltpu.VMEM((X * Y * C, KVL, G, R, D), bf16),
            pltpu.VMEM((Z, X, Y, C, 2, KVL, R, D), bf16),
            pltpu.VMEM((X, KVL, Y, C, G, R, D), bf16),
            pltpu.VMEM((X, KVL, Y, rows, D), f32),
            pltpu.VMEM((X, KVL, Y, rows, D), f32),
            pltpu.VMEM((X, KVL, Y, rows, D), f32),
            pltpu.VMEM((X, Y, rows, D), jnp.int32),
            pltpu.VMEM((X, Y, C, KVL, G, R, D), bf16),
            dma((X, Y, C)),
            dma((X, Y, C)),
            dma((X, Y, C)),
            dma((X, Y, C)),
            dma((2, Z, X, Y)),
            dma((Z, X, Y)),
            dma((Y, C, X)),
            dma((Y, C, X)),
        ],
        compiler_params=pltpu.CompilerParams(
            collective_id=0, has_side_effects=True, vmem_limit_bytes=60 * 2**20
        ),
    )(run_index, freqs, queries, keys, values)
    return jnp.transpose(out.reshape(Y * C * KVL * G, X * R, D), (1, 0, 2))


def solution(mesh):
    in_specs = (
        P("heads", ("team", "blk"), None, None),
        P("heads", ("team", "blk"), None, None),
        P("heads", ("team", "blk"), None, None),
        P(),
    )
    out_specs = P(("team", "blk"), "heads", None)
    return jax.shard_map(
        per_device, mesh=mesh, in_specs=in_specs, out_specs=out_specs, check_vma=False
    )
```

```python
import functools
import math

import jax
import jax.numpy as jnp
import numpy as np
from jax import lax
from jax.experimental import pallas as pl
from jax.experimental.pallas import tpu as pltpu
from jax.sharding import PartitionSpec as P

mask_floor = -1e30
rope_theta = 500000.0
rope_factor = 8.0
low_factor = 1.0
high_factor = 4.0
initial_context = 8192.0


def inverse_freqs(head_width):
    counter = np.arange(head_width // 2, dtype=np.float64)
    base_freq = 1.0 / rope_theta ** (2.0 * counter / head_width)
    wavelength = 2.0 * np.pi / base_freq
    smooth = (initial_context / wavelength - low_factor) / (high_factor - low_factor)
    blended = (1.0 - smooth) * base_freq / rope_factor + smooth * base_freq
    middle = np.where(wavelength > initial_context / low_factor, base_freq / rope_factor, blended)
    return np.where(wavelength < initial_context / high_factor, base_freq, middle)


def small_loop(first, last, body):
    if last - first <= 4:
        for at in range(first, last):
            body(at)
    else:
        lax.fori_loop(first, last, lambda at, unused: (body(at), unused)[1], 0)


def attend_kernel(
    dims,
    run_hbm,
    freq_hbm,
    q_hbm,
    k_hbm,
    v_hbm,
    out_ref,
    run_ref,
    freq_ref,
    q_ref,
    k_ref,
    v_ref,
    load_sem,
    kv_out,
    q_out,
    kv_all,
    q_all,
    acc_ref,
    max_ref,
    sum_ref,
    pos_ref,
    out_part,
    kv_send,
    kv_recv,
    q_send,
    q_recv,
    z_send,
    z_recv,
    o_send,
    o_recv,
):
    X, C, Z, Y, R, KVL, G, D = dims
    S = C * Z * Y
    half = X * R // 2
    rows = C * G * R
    x, c, b = lax.axis_index("heads"), lax.axis_index("team"), lax.axis_index("blk")
    z, y = b // Y, b % Y
    mine = (x * Y + y) * C + c
    def device(xx, cc, bb):
        return {"heads": xx, "team": cc, "blk": bb}

    loads = [
        pltpu.make_async_copy(src, dst, load_sem.at[at])
        for at, (src, dst) in enumerate(
            [(run_hbm, run_ref), (freq_hbm, freq_ref), (k_hbm, k_ref), (v_hbm, v_ref), (q_hbm, q_ref)]
        )
    ]
    for load in loads:
        load.start()

    whole_way = (Z - 1) // 2
    up, down = (z + 1) % Z, (z + Z - 1) % Z

    def below(d):
        return (z + Z - d) % Z

    def above(d):
        return (z + d) % Z

    offsets = [
        (dx, dy, dc)
        for dx in range(X)
        for dy in range(Y)
        for dc in range(C)
        if (dx, dy, dc) != (0, 0, 0)
    ]

    barrier = pltpu.get_barrier_semaphore()

    def greet(xx, cc, bb):
        pl.semaphore_signal(
            barrier, inc=1, device_id=device(xx, cc, bb), device_id_type=pl.DeviceIdType.MESH
        )

    def member(dx, dy, dc):
        return (x + dx) % X, (y + dy) % Y, (c + dc) % C

    for offset in offsets:
        xx, yy, cc = member(*offset)
        greet(xx, cc, z * Y + yy)
    if Z > 1:
        greet(x, c, up * Y + y)
        greet(x, c, down * Y + y)

    def first_pos(slot, piece):
        run = run_ref[slot]
        start = piece * R
        if isinstance(piece, int):
            return run * half + start if start < half else (2 * S - 1 - run) * half + start - half
        return jnp.where(start < half, run * half, (2 * S - 1 - run) * half - half) + start

    loads[0].wait()
    loads[1].wait()

    own_first = first_pos(c * (Z * Y) + b, x)
    pos = own_first + lax.broadcasted_iota(jnp.int32, (R, D), 0)
    angles = pos.astype(jnp.float32) * freq_ref[...]
    cosine = jnp.cos(angles)
    sine = jnp.sin(angles)
    lanes = lax.broadcasted_iota(jnp.int32, (R, D), 1)
    sine = jnp.where(lanes < D // 2, -sine, sine)

    def by_head(ref, first, count):
        return jnp.swapaxes(ref[0, :, first : first + count, :].astype(jnp.float32), 0, 1)

    def rotated(values):
        turned = pltpu.roll(values, D // 2, 2)
        return values * cosine[None] + turned * sine[None]

    loads[2].wait()
    loads[3].wait()
    kv_heads = X * Y * C * KVL
    kv_out[:, 0] = (
        rotated(by_head(k_ref, 0, kv_heads)).astype(jnp.bfloat16).reshape(X * Y * C, KVL, R, D)
    )
    kv_out[:, 1] = by_head(v_ref, 0, kv_heads).astype(jnp.bfloat16).reshape(X * Y * C, KVL, R, D)
    kv_all[z, x, y, c] = kv_out[mine]

    pl.semaphore_wait(barrier, len(offsets) + (2 if Z > 1 else 0))

    def remote(src, dst, send, recv, to):
        return pltpu.make_async_remote_copy(
            src_ref=src,
            dst_ref=dst,
            send_sem=send,
            recv_sem=recv,
            device_id=to,
            device_id_type=pl.DeviceIdType.MESH,
        )

    units_here = [((x + X - dx) % X, (y + Y - dy) % Y) for dx in range(X) for dy in range(Y)]

    def z_copy(at, upward, unit):
        return remote(
            kv_all.at[at, *unit],
            kv_all.at[at, *unit],
            z_send.at[upward, at, *unit],
            z_recv.at[at, *unit],
            device(x, c, (up if upward else down) * Y + y),
        )

    def goes(d, upward, j):
        return d <= whole_way or (2 * d == Z and j % 2 == 1 - upward)

    def pass_on(at, d, upward, j):
        if isinstance(d, int):
            if goes(d, upward, j):
                z_copy(at, upward, units_here[j]).start()
        else:
            here = (d <= whole_way) | ((2 * d == Z) & (j % 2 == 1 - upward))
            pl.when(here)(lambda: z_copy(at, upward, units_here[j]).start())

    def kv_copy(*offset):
        xx, yy, cc = member(*offset)
        return remote(
            kv_out.at[(xx * Y + yy) * C + cc],
            kv_all.at[z, x, y, c],
            kv_send.at[*offset],
            kv_recv.at[*offset],
            device(xx, cc, z * Y + yy),
        )

    def q_copy(*offset):
        xx, yy, cc = member(*offset)
        return remote(
            q_out.at[(xx * Y + yy) * C + cc],
            q_all.at[x, :, y, c],
            q_send.at[*offset],
            q_recv.at[*offset],
            device(xx, cc, z * Y + yy),
        )

    for offset in offsets:
        kv_copy(*offset).start()

    loads[4].wait()
    q_heads = KVL * G
    for to in range(X * Y * C):
        q_out[to] = (
            rotated(by_head(q_ref, to * q_heads, q_heads))
            .astype(jnp.bfloat16)
            .reshape(KVL, G, R, D)
        )
    q_all[x, :, y, c] = q_out[mine]
    for offset in offsets:
        q_copy(*offset).start()
    for dx in range(X):
        for dy in range(Y):
            for dc in range(C):
                if (dx, dy, dc) != (0, 0, 0):
                    kv_copy(dx, dy, dc).wait_recv()
            pass_on(z, 1, 1, dx * Y + dy)
            pass_on(z, 1, 0, dx * Y + dy)

    def receive(d):
        for j, unit in enumerate(units_here):
            z_copy(below(d), 1, unit).wait_recv()
            pass_on(below(d), d + 1, 1, j)
            z_copy(above(d), 0, unit).wait_recv()
            pass_on(above(d), d + 1, 0, j)

    scaling = math.log2(math.e) * D ** (-0.5)

    def key_positions(planes, pieces):
        count = len(pieces) * len(planes) * Y * C * R
        lane = lax.broadcasted_iota(jnp.int32, (1, count), 1)
        segment = lane // R
        total = lane % R
        at = 0
        for piece in pieces:
            for plane in planes:
                for yy in range(Y):
                    for cc in range(C):
                        slot = cc * (Z * Y) + plane * Y + yy
                        total = total + jnp.where(segment == at, first_pos(slot, piece), 0)
                        at += 1
        return total

    def query_positions(piece, yy):
        row = lax.broadcasted_iota(jnp.int32, (rows, D), 0)
        total = row % R
        for cc in range(C):
            slot = cc * (Z * Y) + z * Y + yy
            total = total + jnp.where(row // (G * R) == cc, first_pos(slot, piece), 0)
        return total

    for piece in range(X):
        for yy in range(Y):
            pos_ref[piece, yy] = query_positions(piece, yy)

    early = list(range(X // 2))
    late = list(range(X // 2, X))

    def attend(planes, first, last):

        def units(kind, head, pieces):
            return jnp.concatenate(
                [
                    kv_all[plane, p, yy, cc, kind, head]
                    for p in pieces
                    for plane in planes
                    for yy in range(Y)
                    for cc in range(C)
                ],
                axis=0,
            )

        if planes:
            key_pos = {"early": key_positions(planes, early), "late": key_positions(planes, late)}
        for dy in reversed(range(Y)):
            yy = (y + dy) % Y
            for piece in range(X):
                own = "early" if piece in early else "late"
                parts = ["early"] if own == "early" else ["early", "late"]
                for head in range(KVL):
                    if planes:
                        query = q_all[piece, head, yy].reshape(rows, D)
                        scores = []
                        for part in parts:
                            s = lax.dot_general(
                                query,
                                units(0, head, early if part == "early" else late),
                                (((1,), (1,)), ((), ())),
                                preferred_element_type=jnp.float32,
                            )
                            width = math.gcd(s.shape[1], D)
                            for start in range(0, s.shape[1], width):
                                column = s[:, start : start + width]
                                if part == own:
                                    seen_to = pos_ref[piece, yy, :, :width]
                                    seen = key_pos[part][:, start : start + width] <= seen_to
                                    column = jnp.where(seen, column, mask_floor)
                                scores.append(column)
                        top = jnp.max(functools.reduce(jnp.maximum, scores), axis=-1, keepdims=True)
                        top = jnp.broadcast_to(top, (rows, D))
                        if not first:
                            before = max_ref[piece, head, yy]
                            top = jnp.maximum(top, before)
                            factor = jnp.exp2((before - top) * scaling)
                        weights = [jnp.exp2((s - top[:, :width]) * scaling) for s in scores]
                        total = sum(weights)
                        shared = units(1, head, early if own == "early" else early + late)
                        if width == D:
                            weights = [jnp.concatenate([w.astype(jnp.bfloat16) for w in weights], axis=1)]
                        else:
                            total = jnp.concatenate([total, jnp.zeros((rows, D - width), total.dtype)], axis=1)
                        update, start = 0.0, 0
                        for w in weights:
                            update = update + jnp.dot(
                                w.astype(jnp.bfloat16),
                                shared[start : start + w.shape[1]],
                                preferred_element_type=jnp.float32,
                            )
                            start += w.shape[1]
                        if not first:
                            total = total + sum_ref[piece, head, yy] * factor
                            update = update + acc_ref[piece, head, yy] * factor
                    else:
                        total, update = sum_ref[piece, head, yy], acc_ref[piece, head, yy]
                    if last:
                        mixed = update / jnp.sum(total, axis=-1, keepdims=True)
                        out_part[piece, yy, :, head] = mixed.astype(jnp.bfloat16).reshape(
                            C, G, R, D
                        )
                    else:
                        max_ref[piece, head, yy] = top
                        sum_ref[piece, head, yy] = total
                        acc_ref[piece, head, yy] = update
                if last:
                    for dc in reversed(range(C)):
                        if (dy, dc) != (0, 0):
                            o_copy(dy, dc, piece).start()
                        else:
                            out_ref[y * C + c, :, :, pl.ds(piece * R, R)] = out_part[piece, y, c]

    def o_copy(dy, dc, piece):
        xx, yy, cc = member(0, dy, dc)
        return remote(
            out_part.at[piece, yy, cc],
            out_ref.at[y * C + c, :, :, pl.ds(piece * R, R)],
            o_send.at[dy, dc, piece],
            o_recv.at[dy, dc, piece],
            device(x, cc, z * Y + yy),
        )

    if whole_way > 0:
        receive(1)
    for offset in offsets:
        q_copy(*offset).wait_recv()
    attend([z] + [below(1), above(1)] * min(1, whole_way), True, Z == 1)

    def later(d):
        receive(d)
        attend([below(d), above(d)], False, False)

    small_loop(2, whole_way + 1, later)
    if Z % 2 == 0:
        opposite = above(Z // 2)
        for j, unit in enumerate(units_here):
            z_copy(opposite, 1 - j % 2, unit).wait_recv()
        attend([opposite], False, True)
    elif Z > 1:
        attend([], False, True)

    for offset in offsets:
        kv_copy(*offset).wait_send()
        q_copy(*offset).wait_send()
    def sent(d):
        for j, unit in enumerate(units_here):
            z_copy(below(d), 1, unit).wait_send()
            z_copy(above(d), 0, unit).wait_send()

    small_loop(0, whole_way, sent)
    if Z % 2 == 0:
        for j, unit in enumerate(units_here):
            if j % 2 == 0:
                z_copy(below(Z // 2 - 1), 1, unit).wait_send()
            else:
                z_copy(above(Z // 2 - 1), 0, unit).wait_send()
    for dx, dy, dc in offsets:
        if dx == 0:
            for piece in range(X):
                o_copy(dy, dc, piece).wait()


def per_device(queries, keys, values, run_index):
    X, C, B = lax.axis_size("heads"), lax.axis_size("team"), lax.axis_size("blk")
    R, QH, D = queries.shape[1:]
    KVH = keys.shape[2]
    Y = math.gcd(KVH // (X * C), B)
    KVL = KVH // (X * C * Y)
    G = QH // KVH
    Z = B // Y
    freqs = inverse_freqs(D)
    freqs = jnp.asarray(np.concatenate([freqs, freqs])[None], jnp.float32)
    rows = C * G * R
    hbm = pl.BlockSpec(memory_space=pltpu.HBM)
    dma = pltpu.SemaphoreType.DMA
    bf16, f32 = jnp.bfloat16, jnp.float32
    out = pl.pallas_call(
        functools.partial(attend_kernel, (X, C, Z, Y, R, KVL, G, D)),
        out_shape=pltpu.VMEM((Y * C, KVL, G, X * R, D), bf16),
        in_specs=[hbm] * 5,
        out_specs=pl.BlockSpec(memory_space=pltpu.VMEM),
        scratch_shapes=[
            pltpu.SMEM(run_index.shape, run_index.dtype),
            pltpu.VMEM(freqs.shape, f32),
            pltpu.VMEM(queries.shape, bf16),
            pltpu.VMEM(keys.shape, bf16),
            pltpu.VMEM(values.shape, bf16),
            dma((5,)),
            pltpu.VMEM((X * Y * C, 2, KVL, R, D), bf16),
            pltpu.VMEM((X * Y * C, KVL, G, R, D), bf16),
            pltpu.VMEM((Z, X, Y, C, 2, KVL, R, D), bf16),
            pltpu.VMEM((X, KVL, Y, C, G, R, D), bf16),
            pltpu.VMEM((X, KVL, Y, rows, D), f32),
            pltpu.VMEM((X, KVL, Y, rows, D), f32),
            pltpu.VMEM((X, KVL, Y, rows, D), f32),
            pltpu.VMEM((X, Y, rows, D), jnp.int32),
            pltpu.VMEM((X, Y, C, KVL, G, R, D), bf16),
            dma((X, Y, C)),
            dma((X, Y, C)),
            dma((X, Y, C)),
            dma((X, Y, C)),
            dma((2, Z, X, Y)),
            dma((Z, X, Y)),
            dma((Y, C, X)),
            dma((Y, C, X)),
        ],
        compiler_params=pltpu.CompilerParams(
            collective_id=0, has_side_effects=True, vmem_limit_bytes=60 * 2**20
        ),
    )(run_index, freqs, queries, keys, values)
    return jnp.transpose(out.reshape(Y * C * KVL * G, X * R, D), (1, 0, 2))


def solution(mesh):
    in_specs = (
        P("heads", ("team", "blk"), None, None),
        P("heads", ("team", "blk"), None, None),
        P("heads", ("team", "blk"), None, None),
        P(),
    )
    out_specs = P(("team", "blk"), "heads", None)
    return jax.shard_map(
        per_device, mesh=mesh, in_specs=in_specs, out_specs=out_specs, check_vma=False
    )
```

```python
import functools
import math

import jax
import jax.numpy as jnp
import numpy as np
from jax import lax
from jax.experimental import pallas as pl
from jax.experimental.pallas import tpu as pltpu
from jax.sharding import PartitionSpec as P

mask_floor = -1e30
rope_theta = 500000.0
rope_factor = 8.0
low_factor = 1.0
high_factor = 4.0
initial_context = 8192.0


def inverse_freqs(head_width):
    counter = np.arange(head_width // 2, dtype=np.float64)
    base_freq = 1.0 / rope_theta ** (2.0 * counter / head_width)
    wavelength = 2.0 * np.pi / base_freq
    smooth = (initial_context / wavelength - low_factor) / (high_factor - low_factor)
    blended = (1.0 - smooth) * base_freq / rope_factor + smooth * base_freq
    middle = np.where(wavelength > initial_context / low_factor, base_freq / rope_factor, blended)
    return np.where(wavelength < initial_context / high_factor, base_freq, middle)


def small_loop(first, last, body):
    if last - first <= 4:
        for at in range(first, last):
            body(at)
    else:
        lax.fori_loop(first, last, lambda at, unused: (body(at), unused)[1], 0)


def attend_kernel(
    dims,
    run_hbm,
    freq_hbm,
    q_hbm,
    k_hbm,
    v_hbm,
    out_ref,
    run_ref,
    freq_ref,
    q_ref,
    k_ref,
    v_ref,
    load_sem,
    kv_out,
    q_out,
    kv_all,
    q_all,
    acc_ref,
    max_ref,
    sum_ref,
    pos_ref,
    out_part,
    kv_send,
    kv_recv,
    q_send,
    q_recv,
    z_send,
    z_recv,
    o_send,
    o_recv,
):
    X, C, Z, Y, R, KVL, G, D = dims
    S = C * Z * Y
    half = X * R // 2
    rows = C * G * R
    x, c, b = lax.axis_index("heads"), lax.axis_index("team"), lax.axis_index("blk")
    z, y = b // Y, b % Y
    mine = (x * Y + y) * C + c
    def device(xx, cc, bb):
        return {"heads": xx, "team": cc, "blk": bb}

    loads = [
        pltpu.make_async_copy(src, dst, load_sem.at[at])
        for at, (src, dst) in enumerate(
            [(run_hbm, run_ref), (freq_hbm, freq_ref), (k_hbm, k_ref), (v_hbm, v_ref), (q_hbm, q_ref)]
        )
    ]
    for load in loads:
        load.start()

    whole_way = (Z - 1) // 2
    up, down = (z + 1) % Z, (z + Z - 1) % Z

    def below(d):
        return (z + Z - d) % Z

    def above(d):
        return (z + d) % Z

    offsets = [
        (dx, dy, dc)
        for dx in range(X)
        for dy in range(Y)
        for dc in range(C)
        if (dx, dy, dc) != (0, 0, 0)
    ]

    barrier = pltpu.get_barrier_semaphore()

    def greet(xx, cc, bb):
        pl.semaphore_signal(
            barrier, inc=1, device_id=device(xx, cc, bb), device_id_type=pl.DeviceIdType.MESH
        )

    def member(dx, dy, dc):
        return (x + dx) % X, (y + dy) % Y, (c + dc) % C

    for offset in offsets:
        xx, yy, cc = member(*offset)
        greet(xx, cc, z * Y + yy)
    if Z > 1:
        greet(x, c, up * Y + y)
        greet(x, c, down * Y + y)

    def first_pos(slot, piece):
        run = run_ref[slot]
        start = piece * R
        if isinstance(piece, int):
            return run * half + start if start < half else (2 * S - 1 - run) * half + start - half
        return jnp.where(start < half, run * half, (2 * S - 1 - run) * half - half) + start

    loads[0].wait()
    loads[1].wait()

    own_first = first_pos(c * (Z * Y) + b, x)
    pos = own_first + lax.broadcasted_iota(jnp.int32, (R, D), 0)
    angles = pos.astype(jnp.float32) * freq_ref[...]
    cosine = jnp.cos(angles)
    sine = jnp.sin(angles)
    lanes = lax.broadcasted_iota(jnp.int32, (R, D), 1)
    sine = jnp.where(lanes < D // 2, -sine, sine)

    def by_head(ref, first, count):
        return jnp.swapaxes(ref[0, :, first : first + count, :].astype(jnp.float32), 0, 1)

    def rotated(values):
        turned = pltpu.roll(values, D // 2, 2)
        return values * cosine[None] + turned * sine[None]

    loads[2].wait()
    loads[3].wait()
    kv_heads = X * Y * C * KVL
    kv_out[:, 0] = (
        rotated(by_head(k_ref, 0, kv_heads)).astype(jnp.bfloat16).reshape(X * Y * C, KVL, R, D)
    )
    kv_out[:, 1] = by_head(v_ref, 0, kv_heads).astype(jnp.bfloat16).reshape(X * Y * C, KVL, R, D)
    kv_all[z, x, y, c] = kv_out[mine]

    pl.semaphore_wait(barrier, len(offsets) + (2 if Z > 1 else 0))

    def remote(src, dst, send, recv, to):
        return pltpu.make_async_remote_copy(
            src_ref=src,
            dst_ref=dst,
            send_sem=send,
            recv_sem=recv,
            device_id=to,
            device_id_type=pl.DeviceIdType.MESH,
        )

    units_here = [((x + X - dx) % X, (y + Y - dy) % Y) for dx in range(X) for dy in range(Y)]

    def z_copy(at, upward, unit):
        return remote(
            kv_all.at[at, *unit],
            kv_all.at[at, *unit],
            z_send.at[upward, at, *unit],
            z_recv.at[at, *unit],
            device(x, c, (up if upward else down) * Y + y),
        )

    def goes(d, upward, j):
        return d <= whole_way or (2 * d == Z and j % 2 == 1 - upward)

    def pass_on(at, d, upward, j):
        if isinstance(d, int):
            if goes(d, upward, j):
                z_copy(at, upward, units_here[j]).start()
        else:
            here = (d <= whole_way) | ((2 * d == Z) & (j % 2 == 1 - upward))
            pl.when(here)(lambda: z_copy(at, upward, units_here[j]).start())

    def kv_copy(*offset):
        xx, yy, cc = member(*offset)
        return remote(
            kv_out.at[(xx * Y + yy) * C + cc],
            kv_all.at[z, x, y, c],
            kv_send.at[*offset],
            kv_recv.at[*offset],
            device(xx, cc, z * Y + yy),
        )

    def q_copy(*offset):
        xx, yy, cc = member(*offset)
        return remote(
            q_out.at[(xx * Y + yy) * C + cc],
            q_all.at[x, :, y, c],
            q_send.at[*offset],
            q_recv.at[*offset],
            device(xx, cc, z * Y + yy),
        )

    for offset in offsets:
        kv_copy(*offset).start()

    loads[4].wait()
    q_heads = KVL * G
    for to in range(X * Y * C):
        q_out[to] = (
            rotated(by_head(q_ref, to * q_heads, q_heads))
            .astype(jnp.bfloat16)
            .reshape(KVL, G, R, D)
        )
    q_all[x, :, y, c] = q_out[mine]
    for offset in offsets:
        q_copy(*offset).start()
    for dx in range(X):
        for dy in range(Y):
            for dc in range(C):
                if (dx, dy, dc) != (0, 0, 0):
                    kv_copy(dx, dy, dc).wait_recv()
            pass_on(z, 1, 1, dx * Y + dy)
            pass_on(z, 1, 0, dx * Y + dy)

    def receive(d):
        for j, unit in enumerate(units_here):
            z_copy(below(d), 1, unit).wait_recv()
            pass_on(below(d), d + 1, 1, j)
            z_copy(above(d), 0, unit).wait_recv()
            pass_on(above(d), d + 1, 0, j)

    scaling = math.log2(math.e) * D ** (-0.5)

    def key_positions(planes, pieces):
        count = len(pieces) * len(planes) * Y * C * R
        lane = lax.broadcasted_iota(jnp.int32, (1, count), 1)
        segment = lane // R
        total = lane % R
        at = 0
        for piece in pieces:
            for plane in planes:
                for yy in range(Y):
                    for cc in range(C):
                        slot = cc * (Z * Y) + plane * Y + yy
                        total = total + jnp.where(segment == at, first_pos(slot, piece), 0)
                        at += 1
        return total

    def query_positions(piece, yy, cc):
        row = lax.broadcasted_iota(jnp.int32, (R, D), 0)
        return row + first_pos(cc * (Z * Y) + z * Y + yy, piece)

    for piece in range(X):
        for yy in range(Y):
            for cc in range(C):
                pos_ref[piece, yy, cc] = query_positions(piece, yy, cc)

    early = list(range(X // 2))
    late = list(range(X // 2, X))

    def attend(planes, first, last):

        def units(kind, head, pieces):
            return jnp.concatenate(
                [
                    kv_all[plane, p, yy, cc, kind, head]
                    for p in pieces
                    for plane in planes
                    for yy in range(Y)
                    for cc in range(C)
                ],
                axis=0,
            )

        if planes:
            key_pos = {"early": key_positions(planes, early), "late": key_positions(planes, late)}
        for dy in reversed(range(Y)):
            yy = (y + dy) % Y
            for piece in range(X):
                own = "early" if piece in early else "late"
                parts = ["early"] if own == "early" else ["early", "late"]
                for head in range(KVL):
                    if planes:
                        query = q_all[piece, head, yy].reshape(rows, D)
                        scores = [
                            lax.dot_general(
                                query,
                                units(0, head, early if part == "early" else late),
                                (((1,), (1,)), ((), ())),
                                preferred_element_type=jnp.float32,
                            )
                            for part in parts
                        ]
                        width = math.gcd(scores[0].shape[1], D)
                        rounded, totals, factors = [], [], []
                        for at in range(0, rows, R):
                            block = slice(at, at + R)
                            seen_to = pos_ref[piece, yy, at // (G * R), :, :width]
                            columns = []
                            for part, s in zip(parts, scores):
                                for start in range(0, s.shape[1], width):
                                    column = s[block, start : start + width]
                                    if part == own:
                                        seen = key_pos[part][:, start : start + width] <= seen_to
                                        column = jnp.where(seen, column, mask_floor)
                                    columns.append(column)
                            top = jnp.max(
                                functools.reduce(jnp.maximum, columns), axis=-1, keepdims=True
                            )
                            top = jnp.broadcast_to(top, (R, D))
                            if not first:
                                before = max_ref[piece, head, yy, block]
                                top = jnp.maximum(top, before)
                                factors.append(jnp.exp2((before - top) * scaling))
                            weights = [jnp.exp2((s - top[:, :width]) * scaling) for s in columns]
                            total = sum(weights)
                            if width < D:
                                filler = jnp.zeros((R, D - width), total.dtype)
                                total = jnp.concatenate([total, filler], axis=1)
                            if not first:
                                total = total + sum_ref[piece, head, yy, block] * factors[-1]
                            totals.append(total)
                            rounded.append([w.astype(jnp.bfloat16) for w in weights])
                            if not last:
                                max_ref[piece, head, yy, block] = top
                        weights = [jnp.concatenate(ws, axis=0) for ws in zip(*rounded)]
                        if width == D:
                            weights = [jnp.concatenate(weights, axis=1)]
                        total = jnp.concatenate(totals, axis=0)
                        shared = units(1, head, early if own == "early" else early + late)
                        update, start = 0.0, 0
                        for w in weights:
                            update = update + jnp.dot(
                                w,
                                shared[start : start + w.shape[1]],
                                preferred_element_type=jnp.float32,
                            )
                            start += w.shape[1]
                        if not first:
                            factor = jnp.concatenate(factors, axis=0)
                            update = update + acc_ref[piece, head, yy] * factor
                    else:
                        total, update = sum_ref[piece, head, yy], acc_ref[piece, head, yy]
                    if last:
                        mixed = update * (1.0 / jnp.sum(total, axis=-1, keepdims=True))
                        out_part[piece, yy, :, head] = mixed.astype(jnp.bfloat16).reshape(
                            C, G, R, D
                        )
                    else:
                        sum_ref[piece, head, yy] = total
                        acc_ref[piece, head, yy] = update
                if last:
                    for dc in reversed(range(C)):
                        if (dy, dc) != (0, 0):
                            o_copy(dy, dc, piece).start()
                        else:
                            out_ref[y * C + c, :, :, pl.ds(piece * R, R)] = out_part[piece, y, c]

    def o_copy(dy, dc, piece):
        xx, yy, cc = member(0, dy, dc)
        return remote(
            out_part.at[piece, yy, cc],
            out_ref.at[y * C + c, :, :, pl.ds(piece * R, R)],
            o_send.at[dy, dc, piece],
            o_recv.at[dy, dc, piece],
            device(x, cc, z * Y + yy),
        )

    if whole_way > 0:
        receive(1)
    for offset in offsets:
        q_copy(*offset).wait_recv()
    attend([z] + [below(1), above(1)] * min(1, whole_way), True, Z == 1)

    def later(d):
        receive(d)
        attend([below(d), above(d)], False, False)

    small_loop(2, whole_way + 1, later)
    if Z % 2 == 0:
        opposite = above(Z // 2)
        for j, unit in enumerate(units_here):
            z_copy(opposite, 1 - j % 2, unit).wait_recv()
        attend([opposite], False, True)
    elif Z > 1:
        attend([], False, True)

    for offset in offsets:
        kv_copy(*offset).wait_send()
        q_copy(*offset).wait_send()
    def sent(d):
        for j, unit in enumerate(units_here):
            z_copy(below(d), 1, unit).wait_send()
            z_copy(above(d), 0, unit).wait_send()

    small_loop(0, whole_way, sent)
    if Z % 2 == 0:
        for j, unit in enumerate(units_here):
            if j % 2 == 0:
                z_copy(below(Z // 2 - 1), 1, unit).wait_send()
            else:
                z_copy(above(Z // 2 - 1), 0, unit).wait_send()
    for dx, dy, dc in offsets:
        if dx == 0:
            for piece in range(X):
                o_copy(dy, dc, piece).wait()


def per_device(queries, keys, values, run_index):
    X, C, B = lax.axis_size("heads"), lax.axis_size("team"), lax.axis_size("blk")
    R, QH, D = queries.shape[1:]
    KVH = keys.shape[2]
    Y = math.gcd(KVH // (X * C), B)
    KVL = KVH // (X * C * Y)
    G = QH // KVH
    Z = B // Y
    freqs = inverse_freqs(D)
    freqs = jnp.asarray(np.concatenate([freqs, freqs])[None], jnp.float32)
    rows = C * G * R
    hbm = pl.BlockSpec(memory_space=pltpu.HBM)
    dma = pltpu.SemaphoreType.DMA
    bf16, f32 = jnp.bfloat16, jnp.float32
    out = pl.pallas_call(
        functools.partial(attend_kernel, (X, C, Z, Y, R, KVL, G, D)),
        out_shape=pltpu.VMEM((Y * C, KVL, G, X * R, D), bf16),
        in_specs=[hbm] * 5,
        out_specs=pl.BlockSpec(memory_space=pltpu.VMEM),
        scratch_shapes=[
            pltpu.SMEM(run_index.shape, run_index.dtype),
            pltpu.VMEM(freqs.shape, f32),
            pltpu.VMEM(queries.shape, bf16),
            pltpu.VMEM(keys.shape, bf16),
            pltpu.VMEM(values.shape, bf16),
            dma((5,)),
            pltpu.VMEM((X * Y * C, 2, KVL, R, D), bf16),
            pltpu.VMEM((X * Y * C, KVL, G, R, D), bf16),
            pltpu.VMEM((Z, X, Y, C, 2, KVL, R, D), bf16),
            pltpu.VMEM((X, KVL, Y, C, G, R, D), bf16),
            pltpu.VMEM((X, KVL, Y, rows, D), f32),
            pltpu.VMEM((X, KVL, Y, rows, D), f32),
            pltpu.VMEM((X, KVL, Y, rows, D), f32),
            pltpu.VMEM((X, Y, C, R, D), jnp.int32),
            pltpu.VMEM((X, Y, C, KVL, G, R, D), bf16),
            dma((X, Y, C)),
            dma((X, Y, C)),
            dma((X, Y, C)),
            dma((X, Y, C)),
            dma((2, Z, X, Y)),
            dma((Z, X, Y)),
            dma((Y, C, X)),
            dma((Y, C, X)),
        ],
        compiler_params=pltpu.CompilerParams(
            collective_id=0, has_side_effects=True, vmem_limit_bytes=60 * 2**20
        ),
    )(run_index, freqs, queries, keys, values)
    return jnp.transpose(out.reshape(Y * C * KVL * G, X * R, D), (1, 0, 2))


def solution(mesh):
    in_specs = (
        P("heads", ("team", "blk"), None, None),
        P("heads", ("team", "blk"), None, None),
        P("heads", ("team", "blk"), None, None),
        P(),
    )
    out_specs = P(("team", "blk"), "heads", None)
    return jax.shard_map(
        per_device, mesh=mesh, in_specs=in_specs, out_specs=out_specs, check_vma=False
    )
```

```python
import functools
import math

import jax
import jax.numpy as jnp
import numpy as np
from jax import lax
from jax.experimental import pallas as pl
from jax.experimental.pallas import tpu as pltpu
from jax.sharding import PartitionSpec as P

mask_floor = -1e30
rope_theta = 500000.0
rope_factor = 8.0
low_factor = 1.0
high_factor = 4.0
initial_context = 8192.0


def inverse_freqs(head_width):
    counter = np.arange(head_width // 2, dtype=np.float64)
    base_freq = 1.0 / rope_theta ** (2.0 * counter / head_width)
    wavelength = 2.0 * np.pi / base_freq
    smooth = (initial_context / wavelength - low_factor) / (high_factor - low_factor)
    blended = (1.0 - smooth) * base_freq / rope_factor + smooth * base_freq
    middle = np.where(wavelength > initial_context / low_factor, base_freq / rope_factor, blended)
    return np.where(wavelength < initial_context / high_factor, base_freq, middle)


def small_loop(first, last, body):
    if last - first <= 4:
        for at in range(first, last):
            body(at)
    else:
        lax.fori_loop(first, last, lambda at, unused: (body(at), unused)[1], 0)


def attend_kernel(
    dims,
    run_hbm,
    freq_hbm,
    q_hbm,
    k_hbm,
    v_hbm,
    out_ref,
    run_ref,
    freq_ref,
    q_ref,
    k_ref,
    v_ref,
    load_sem,
    kv_out,
    q_out,
    kv_all,
    q_all,
    acc_ref,
    max_ref,
    sum_ref,
    pos_ref,
    out_part,
    kv_send,
    kv_recv,
    q_send,
    q_recv,
    z_send,
    z_recv,
    o_send,
    o_recv,
):
    X, C, Z, Y, R, KVL, G, D = dims
    S = C * Z * Y
    half = X * R // 2
    rows = C * G * R
    x, c, b = lax.axis_index("heads"), lax.axis_index("team"), lax.axis_index("blk")
    z, y = b // Y, b % Y
    mine = (x * Y + y) * C + c
    def device(xx, cc, bb):
        return {"heads": xx, "team": cc, "blk": bb}

    loads = [
        pltpu.make_async_copy(src, dst, load_sem.at[at])
        for at, (src, dst) in enumerate(
            [(run_hbm, run_ref), (freq_hbm, freq_ref), (k_hbm, k_ref), (v_hbm, v_ref), (q_hbm, q_ref)]
        )
    ]
    for load in loads:
        load.start()

    low, high = z, Z - 1 - z
    near = jnp.minimum(low, high)
    between = (low > 0) & (high > 0)

    def z_near(k):
        if isinstance(k, int) and k == 0:
            return z
        paired = jnp.where(k % 2 == 1, z - (k + 1) // 2, z + k // 2)
        single = jnp.where(low < high, z + (k - near), z - (k - near))
        return jnp.where(k <= 2 * near, paired, single)

    offsets = [
        (dx, dy, dc)
        for dx in range(X)
        for dy in range(Y)
        for dc in range(C)
        if (dx, dy, dc) != (0, 0, 0)
    ]

    barrier = pltpu.get_barrier_semaphore()

    def greet(xx, cc, bb):
        pl.semaphore_signal(
            barrier, inc=1, device_id=device(xx, cc, bb), device_id_type=pl.DeviceIdType.MESH
        )

    def member(dx, dy, dc):
        return (x + dx) % X, (y + dy) % Y, (c + dc) % C

    for offset in offsets:
        xx, yy, cc = member(*offset)
        greet(xx, cc, z * Y + yy)
    pl.when(low > 0)(lambda: greet(x, c, b - Y))
    pl.when(high > 0)(lambda: greet(x, c, b + Y))

    def first_pos(slot, piece):
        run = run_ref[slot]
        start = piece * R
        if isinstance(piece, int):
            return run * half + start if start < half else (2 * S - 1 - run) * half + start - half
        return jnp.where(start < half, run * half, (2 * S - 1 - run) * half - half) + start

    loads[0].wait()
    loads[1].wait()

    own_first = first_pos(c * (Z * Y) + b, x)
    pos = own_first + lax.broadcasted_iota(jnp.int32, (R, D), 0)
    angles = pos.astype(jnp.float32) * freq_ref[...]
    cosine = jnp.cos(angles)
    sine = jnp.sin(angles)
    lanes = lax.broadcasted_iota(jnp.int32, (R, D), 1)
    sine = jnp.where(lanes < D // 2, -sine, sine)

    def by_head(ref, first, count):
        return jnp.swapaxes(ref[0, :, first : first + count, :].astype(jnp.float32), 0, 1)

    def rotated(values):
        turned = pltpu.roll(values, D // 2, 2)
        return values * cosine[None] + turned * sine[None]

    loads[2].wait()
    loads[3].wait()
    kv_heads = X * Y * C * KVL
    kv_out[:, 0] = (
        rotated(by_head(k_ref, 0, kv_heads)).astype(jnp.bfloat16).reshape(X * Y * C, KVL, R, D)
    )
    kv_out[:, 1] = by_head(v_ref, 0, kv_heads).astype(jnp.bfloat16).reshape(X * Y * C, KVL, R, D)
    kv_all[z, x, y, c] = kv_out[mine]

    pl.semaphore_wait(barrier, len(offsets) + jnp.minimum(low, 1) + jnp.minimum(high, 1))

    def remote(src, dst, send, recv, to):
        return pltpu.make_async_remote_copy(
            src_ref=src,
            dst_ref=dst,
            send_sem=send,
            recv_sem=recv,
            device_id=to,
            device_id_type=pl.DeviceIdType.MESH,
        )

    units_here = [
        ((x + X - dx) % X, (y + Y - dy) % Y, (c + C - dc) % C)
        for dx in range(X)
        for dy in range(Y)
        for dc in range(C)
    ]

    def z_copy(at, upward, unit):
        return remote(
            kv_all.at[at, *unit],
            kv_all.at[at, *unit],
            z_send.at[upward, at, *unit],
            z_recv.at[at, *unit],
            device(x, c, b + Y if upward else b - Y),
        )

    def pass_on(at, unit):
        pl.when((at <= z) & (high > 0))(lambda: z_copy(at, 1, unit).start())
        pl.when((at >= z) & (low > 0))(lambda: z_copy(at, 0, unit).start())

    def kv_copy(*offset):
        xx, yy, cc = member(*offset)
        return remote(
            kv_out.at[(xx * Y + yy) * C + cc],
            kv_all.at[z, x, y, c],
            kv_send.at[*offset],
            kv_recv.at[*offset],
            device(xx, cc, z * Y + yy),
        )

    def q_copy(*offset):
        xx, yy, cc = member(*offset)
        return remote(
            q_out.at[(xx * Y + yy) * C + cc],
            q_all.at[x, :, y, c],
            q_send.at[*offset],
            q_recv.at[*offset],
            device(xx, cc, z * Y + yy),
        )

    for offset in offsets:
        kv_copy(*offset).start()
    pass_on(z, units_here[0])

    loads[4].wait()
    q_heads = KVL * G
    for to in range(X * Y * C):
        q_out[to] = (
            rotated(by_head(q_ref, to * q_heads, q_heads))
            .astype(jnp.bfloat16)
            .reshape(KVL, G, R, D)
        )
    q_all[x, :, y, c] = q_out[mine]
    for offset in offsets:
        q_copy(*offset).start()
    for offset, unit in zip(offsets, units_here[1:]):
        kv_copy(*offset).wait_recv()
        pass_on(z, unit)

    def receive(k):
        at = z_near(k)
        for unit in units_here:
            z_copy(at, 1, unit).wait_recv()
            pass_on(at, unit)

    scaling = math.log2(math.e) * D ** (-0.5)

    def key_positions(planes, pieces):
        count = len(pieces) * len(planes) * Y * C * R
        lane = lax.broadcasted_iota(jnp.int32, (1, count), 1)
        segment = lane // R
        total = lane % R
        at = 0
        for piece in pieces:
            for plane in planes:
                for yy in range(Y):
                    for cc in range(C):
                        slot = cc * (Z * Y) + plane * Y + yy
                        total = total + jnp.where(segment == at, first_pos(slot, piece), 0)
                        at += 1
        return total

    def query_positions(piece, yy, cc):
        row = lax.broadcasted_iota(jnp.int32, (R, D), 0)
        return row + first_pos(cc * (Z * Y) + z * Y + yy, piece)

    for piece in range(X):
        for yy in range(Y):
            for cc in range(C):
                pos_ref[piece, yy, cc] = query_positions(piece, yy, cc)

    early = list(range(X // 2))
    late = list(range(X // 2, X))

    def attend(planes, first, last):

        def units(kind, head, pieces):
            return jnp.concatenate(
                [
                    kv_all[plane, p, yy, cc, kind, head]
                    for p in pieces
                    for plane in planes
                    for yy in range(Y)
                    for cc in range(C)
                ],
                axis=0,
            )

        if planes:
            key_pos = {"early": key_positions(planes, early), "late": key_positions(planes, late)}
        for dy in reversed(range(Y)):
            yy = (y + dy) % Y
            for piece in range(X):
                own = "early" if piece in early else "late"
                parts = ["early"] if own == "early" else ["early", "late"]
                for head in range(KVL):
                    if planes:
                        query = q_all[piece, head, yy].reshape(rows, D)
                        scores = [
                            lax.dot_general(
                                query,
                                units(0, head, early if part == "early" else late),
                                (((1,), (1,)), ((), ())),
                                preferred_element_type=jnp.float32,
                            )
                            for part in parts
                        ]
                        width = math.gcd(scores[0].shape[1], D)
                        rounded, totals, factors = [], [], []
                        for at in range(0, rows, R):
                            block = slice(at, at + R)
                            seen_to = pos_ref[piece, yy, at // (G * R), :, :width]
                            columns = []
                            for part, s in zip(parts, scores):
                                for start in range(0, s.shape[1], width):
                                    column = s[block, start : start + width]
                                    if part == own:
                                        seen = key_pos[part][:, start : start + width] <= seen_to
                                        column = jnp.where(seen, column, mask_floor)
                                    columns.append(column)
                            top = jnp.max(
                                functools.reduce(jnp.maximum, columns), axis=-1, keepdims=True
                            )
                            top = jnp.broadcast_to(top, (R, D))
                            if not first:
                                before = max_ref[piece, head, yy, block]
                                top = jnp.maximum(top, before)
                                factors.append(jnp.exp2((before - top) * scaling))
                            weights = [jnp.exp2((s - top[:, :width]) * scaling) for s in columns]
                            total = sum(weights)
                            if width < D:
                                filler = jnp.zeros((R, D - width), total.dtype)
                                total = jnp.concatenate([total, filler], axis=1)
                            if not first:
                                total = total + sum_ref[piece, head, yy, block] * factors[-1]
                            totals.append(total)
                            rounded.append([w.astype(jnp.bfloat16) for w in weights])
                            if not last:
                                max_ref[piece, head, yy, block] = top
                        weights = [jnp.concatenate(ws, axis=0) for ws in zip(*rounded)]
                        if width == D:
                            weights = [jnp.concatenate(weights, axis=1)]
                        total = jnp.concatenate(totals, axis=0)
                        shared = units(1, head, early if own == "early" else early + late)
                        update, start = 0.0, 0
                        for w in weights:
                            update = update + jnp.dot(
                                w,
                                shared[start : start + w.shape[1]],
                                preferred_element_type=jnp.float32,
                            )
                            start += w.shape[1]
                        if not first:
                            factor = jnp.concatenate(factors, axis=0)
                            update = update + acc_ref[piece, head, yy] * factor
                    else:
                        total, update = sum_ref[piece, head, yy], acc_ref[piece, head, yy]
                    if last:
                        mixed = update * (1.0 / jnp.sum(total, axis=-1, keepdims=True))
                        out_part[piece, yy, :, head] = mixed.astype(jnp.bfloat16).reshape(
                            C, G, R, D
                        )
                    else:
                        sum_ref[piece, head, yy] = total
                        acc_ref[piece, head, yy] = update
                if last:
                    for dc in reversed(range(C)):
                        if (dy, dc) != (0, 0):
                            o_copy(dy, dc, piece).start()
                        else:
                            out_ref[y * C + c, :, :, pl.ds(piece * R, R)] = out_part[piece, y, c]

    def o_copy(dy, dc, piece):
        xx, yy, cc = member(0, dy, dc)
        return remote(
            out_part.at[piece, yy, cc],
            out_ref.at[y * C + c, :, :, pl.ds(piece * R, R)],
            o_send.at[dy, dc, piece],
            o_recv.at[dy, dc, piece],
            device(x, cc, z * Y + yy),
        )

    small_loop(1, Z - 1, receive)
    if Z > 1:
        pl.when(between)(lambda: receive(Z - 1))
    for offset in offsets:
        q_copy(*offset).wait_recv()
    together = min(3, max(1, Z - 1))
    attend([z_near(k) for k in range(together)], True, Z == 1)
    small_loop(together, Z - 1, lambda k: attend([z_near(k)], False, False))
    if Z > 1:
        pl.when(jnp.logical_not(between))(lambda: receive(Z - 1))
        attend([z_near(Z - 1)], False, True)

    for offset in offsets:
        kv_copy(*offset).wait_send()
        q_copy(*offset).wait_send()
    def sent(at):
        for unit in units_here:
            pl.when((at <= z) & (high > 0))(lambda: z_copy(at, 1, unit).wait_send())
            pl.when((at >= z) & (low > 0))(lambda: z_copy(at, 0, unit).wait_send())

    small_loop(0, Z, sent)
    for dx, dy, dc in offsets:
        if dx == 0:
            for piece in range(X):
                o_copy(dy, dc, piece).wait()


def per_device(queries, keys, values, run_index):
    X, C, B = lax.axis_size("heads"), lax.axis_size("team"), lax.axis_size("blk")
    R, QH, D = queries.shape[1:]
    KVH = keys.shape[2]
    Y = math.gcd(KVH // (X * C), B)
    KVL = KVH // (X * C * Y)
    G = QH // KVH
    Z = B // Y
    freqs = inverse_freqs(D)
    freqs = jnp.asarray(np.concatenate([freqs, freqs])[None], jnp.float32)
    rows = C * G * R
    hbm = pl.BlockSpec(memory_space=pltpu.HBM)
    dma = pltpu.SemaphoreType.DMA
    bf16, f32 = jnp.bfloat16, jnp.float32
    out = pl.pallas_call(
        functools.partial(attend_kernel, (X, C, Z, Y, R, KVL, G, D)),
        out_shape=pltpu.VMEM((Y * C, KVL, G, X * R, D), bf16),
        in_specs=[hbm] * 5,
        out_specs=pl.BlockSpec(memory_space=pltpu.VMEM),
        scratch_shapes=[
            pltpu.SMEM(run_index.shape, run_index.dtype),
            pltpu.VMEM(freqs.shape, f32),
            pltpu.VMEM(queries.shape, bf16),
            pltpu.VMEM(keys.shape, bf16),
            pltpu.VMEM(values.shape, bf16),
            dma((5,)),
            pltpu.VMEM((X * Y * C, 2, KVL, R, D), bf16),
            pltpu.VMEM((X * Y * C, KVL, G, R, D), bf16),
            pltpu.VMEM((Z, X, Y, C, 2, KVL, R, D), bf16),
            pltpu.VMEM((X, KVL, Y, C, G, R, D), bf16),
            pltpu.VMEM((X, KVL, Y, rows, D), f32),
            pltpu.VMEM((X, KVL, Y, rows, D), f32),
            pltpu.VMEM((X, KVL, Y, rows, D), f32),
            pltpu.VMEM((X, Y, C, R, D), jnp.int32),
            pltpu.VMEM((X, Y, C, KVL, G, R, D), bf16),
            dma((X, Y, C)),
            dma((X, Y, C)),
            dma((X, Y, C)),
            dma((X, Y, C)),
            dma((2, Z, X, Y, C)),
            dma((Z, X, Y, C)),
            dma((Y, C, X)),
            dma((Y, C, X)),
        ],
        compiler_params=pltpu.CompilerParams(
            collective_id=0, has_side_effects=True, vmem_limit_bytes=60 * 2**20
        ),
    )(run_index, freqs, queries, keys, values)
    return jnp.transpose(out.reshape(Y * C * KVL * G, X * R, D), (1, 0, 2))


def solution(mesh):
    in_specs = (
        P("heads", ("team", "blk"), None, None),
        P("heads", ("team", "blk"), None, None),
        P("heads", ("team", "blk"), None, None),
        P(),
    )
    out_specs = P(("team", "blk"), "heads", None)
    return jax.shard_map(
        per_device, mesh=mesh, in_specs=in_specs, out_specs=out_specs, check_vma=False
    )
```

```python
import functools
import math

import jax
import jax.numpy as jnp
import numpy as np
from jax import lax
from jax.experimental import pallas as pl
from jax.experimental.pallas import tpu as pltpu
from jax.sharding import PartitionSpec as P

mask_floor = -1e30
rope_theta = 500000.0
rope_factor = 8.0
low_factor = 1.0
high_factor = 4.0
initial_context = 8192.0


def inverse_freqs(head_width):
    counter = np.arange(head_width // 2, dtype=np.float64)
    base_freq = 1.0 / rope_theta ** (2.0 * counter / head_width)
    wavelength = 2.0 * np.pi / base_freq
    smooth = (initial_context / wavelength - low_factor) / (high_factor - low_factor)
    blended = (1.0 - smooth) * base_freq / rope_factor + smooth * base_freq
    middle = np.where(wavelength > initial_context / low_factor, base_freq / rope_factor, blended)
    return np.where(wavelength < initial_context / high_factor, base_freq, middle)


def small_loop(first, last, body):
    if last - first <= 4:
        for at in range(first, last):
            body(at)
    else:
        lax.fori_loop(first, last, lambda at, unused: (body(at), unused)[1], 0)


def attend_kernel(
    dims,
    run_hbm,
    freq_hbm,
    q_hbm,
    k_hbm,
    v_hbm,
    out_ref,
    run_ref,
    freq_ref,
    q_ref,
    k_ref,
    v_ref,
    load_sem,
    kv_out,
    q_out,
    kv_all,
    q_all,
    acc_ref,
    max_ref,
    sum_ref,
    pos_ref,
    out_part,
    kv_send,
    kv_recv,
    q_send,
    q_recv,
    z_send,
    z_recv,
    o_send,
    o_recv,
):
    X, C, Z, Y, R, KVL, G, D = dims
    S = C * Z * Y
    half = X * R // 2
    rows = C * G * R
    x, c, b = lax.axis_index("heads"), lax.axis_index("team"), lax.axis_index("blk")
    z, y = b // Y, b % Y
    mine = (x * Y + y) * C + c
    def device(xx, cc, bb):
        return {"heads": xx, "team": cc, "blk": bb}

    loads = [
        pltpu.make_async_copy(src, dst, load_sem.at[at])
        for at, (src, dst) in enumerate(
            [(run_hbm, run_ref), (freq_hbm, freq_ref), (k_hbm, k_ref), (v_hbm, v_ref), (q_hbm, q_ref)]
        )
    ]
    for load in loads:
        load.start()

    whole_way = (Z - 1) // 2
    up, down = (z + 1) % Z, (z + Z - 1) % Z

    def below(d):
        return (z + Z - d) % Z

    def above(d):
        return (z + d) % Z

    offsets = [
        (dx, dy, dc)
        for dx in range(X)
        for dy in range(Y)
        for dc in range(C)
        if (dx, dy, dc) != (0, 0, 0)
    ]

    barrier = pltpu.get_barrier_semaphore()

    def greet(xx, cc, bb):
        pl.semaphore_signal(
            barrier, inc=1, device_id=device(xx, cc, bb), device_id_type=pl.DeviceIdType.MESH
        )

    def member(dx, dy, dc):
        return (x + dx) % X, (y + dy) % Y, (c + dc) % C

    for offset in offsets:
        xx, yy, cc = member(*offset)
        greet(xx, cc, z * Y + yy)
    if Z > 1:
        greet(x, c, up * Y + y)
        greet(x, c, down * Y + y)

    def first_pos(slot, piece):
        run = run_ref[slot]
        start = piece * R
        if isinstance(piece, int):
            return run * half + start if start < half else (2 * S - 1 - run) * half + start - half
        return jnp.where(start < half, run * half, (2 * S - 1 - run) * half - half) + start

    loads[0].wait()
    loads[1].wait()

    own_first = first_pos(c * (Z * Y) + b, x)
    pos = own_first + lax.broadcasted_iota(jnp.int32, (R, D), 0)
    angles = pos.astype(jnp.float32) * freq_ref[...]
    cosine = jnp.cos(angles)
    sine = jnp.sin(angles)
    lanes = lax.broadcasted_iota(jnp.int32, (R, D), 1)
    sine = jnp.where(lanes < D // 2, -sine, sine)

    def by_head(ref, first, count):
        return jnp.swapaxes(ref[0, :, first : first + count, :].astype(jnp.float32), 0, 1)

    def rotated(values):
        turned = pltpu.roll(values, D // 2, 2)
        return values * cosine[None] + turned * sine[None]

    loads[2].wait()
    loads[3].wait()
    kv_heads = X * Y * C * KVL
    kv_out[:, 0] = (
        rotated(by_head(k_ref, 0, kv_heads)).astype(jnp.bfloat16).reshape(X * Y * C, KVL, R, D)
    )
    kv_out[:, 1] = by_head(v_ref, 0, kv_heads).astype(jnp.bfloat16).reshape(X * Y * C, KVL, R, D)
    kv_all[z, x, y, c] = kv_out[mine]

    pl.semaphore_wait(barrier, len(offsets) + (2 if Z > 1 else 0))

    def remote(src, dst, send, recv, to):
        return pltpu.make_async_remote_copy(
            src_ref=src,
            dst_ref=dst,
            send_sem=send,
            recv_sem=recv,
            device_id=to,
            device_id_type=pl.DeviceIdType.MESH,
        )

    units_here = [((x + X - dx) % X, (y + Y - dy) % Y) for dx in range(X) for dy in range(Y)]

    def z_copy(at, upward, unit):
        return remote(
            kv_all.at[at, *unit],
            kv_all.at[at, *unit],
            z_send.at[upward, at, *unit],
            z_recv.at[at, *unit],
            device(x, c, (up if upward else down) * Y + y),
        )

    def goes(d, upward, j):
        return d <= whole_way or (2 * d == Z and j % 2 == 1 - upward)

    def pass_on(at, d, upward, j):
        if isinstance(d, int):
            if goes(d, upward, j):
                z_copy(at, upward, units_here[j]).start()
        else:
            here = (d <= whole_way) | ((2 * d == Z) & (j % 2 == 1 - upward))
            pl.when(here)(lambda: z_copy(at, upward, units_here[j]).start())

    def kv_copy(*offset):
        xx, yy, cc = member(*offset)
        return remote(
            kv_out.at[(xx * Y + yy) * C + cc],
            kv_all.at[z, x, y, c],
            kv_send.at[*offset],
            kv_recv.at[*offset],
            device(xx, cc, z * Y + yy),
        )

    def q_copy(*offset):
        xx, yy, cc = member(*offset)
        return remote(
            q_out.at[(xx * Y + yy) * C + cc],
            q_all.at[x, :, y, c],
            q_send.at[*offset],
            q_recv.at[*offset],
            device(xx, cc, z * Y + yy),
        )

    for offset in offsets:
        kv_copy(*offset).start()

    loads[4].wait()
    q_heads = KVL * G
    share = math.gcd(X * Y * C, max(1, 8 // q_heads))
    for to in range(0, X * Y * C, share):
        q_out[to : to + share] = (
            rotated(by_head(q_ref, to * q_heads, share * q_heads))
            .astype(jnp.bfloat16)
            .reshape(share, KVL, G, R, D)
        )
    q_all[x, :, y, c] = q_out[mine]
    for offset in offsets:
        q_copy(*offset).start()
    for dx in range(X):
        for dy in range(Y):
            for dc in range(C):
                if (dx, dy, dc) != (0, 0, 0):
                    kv_copy(dx, dy, dc).wait_recv()
            pass_on(z, 1, 1, dx * Y + dy)
            pass_on(z, 1, 0, dx * Y + dy)

    def receive(d):
        for j, unit in enumerate(units_here):
            z_copy(below(d), 1, unit).wait_recv()
            pass_on(below(d), d + 1, 1, j)
            z_copy(above(d), 0, unit).wait_recv()
            pass_on(above(d), d + 1, 0, j)

    scaling = math.log2(math.e) * D ** (-0.5)

    def key_positions(planes, pieces):
        count = len(pieces) * len(planes) * Y * C * R
        lane = lax.broadcasted_iota(jnp.int32, (1, count), 1)
        segment = lane // R
        total = lane % R
        at = 0
        for piece in pieces:
            for plane in planes:
                for yy in range(Y):
                    for cc in range(C):
                        slot = cc * (Z * Y) + plane * Y + yy
                        total = total + jnp.where(segment == at, first_pos(slot, piece), 0)
                        at += 1
        return total

    def query_positions(piece, yy, cc):
        row = lax.broadcasted_iota(jnp.int32, (R, D), 0)
        return row + first_pos(cc * (Z * Y) + z * Y + yy, piece)

    for piece in range(X):
        for yy in range(Y):
            for cc in range(C):
                pos_ref[piece, yy, cc] = query_positions(piece, yy, cc)

    early = list(range(X // 2))
    late = list(range(X // 2, X))

    def attend(planes, first, last):

        def units(kind, head, pieces):
            return jnp.concatenate(
                [
                    kv_all[plane, p, yy, cc, kind, head]
                    for p in pieces
                    for plane in planes
                    for yy in range(Y)
                    for cc in range(C)
                ],
                axis=0,
            )

        if planes:
            key_pos = {"early": key_positions(planes, early), "late": key_positions(planes, late)}
        def blocks_of(step, unused):
            dy = Y - 1 - step
            yy = (y + dy) % Y
            for piece in range(X):
                own = "early" if piece in early else "late"
                parts = ["early"] if own == "early" else ["early", "late"]
                for head in range(KVL):
                    if planes:
                        query = q_all[piece, head, yy].reshape(rows, D)
                        scores = [
                            lax.dot_general(
                                query,
                                units(0, head, early if part == "early" else late),
                                (((1,), (1,)), ((), ())),
                                preferred_element_type=jnp.float32,
                            )
                            for part in parts
                        ]
                        width = math.gcd(scores[0].shape[1], D)
                        rounded, totals, factors = [], [], []
                        for at in range(0, rows, R):
                            block = slice(at, at + R)
                            seen_to = pos_ref[piece, yy, at // (G * R), :, :width]
                            columns = []
                            for part, s in zip(parts, scores):
                                for start in range(0, s.shape[1], width):
                                    column = s[block, start : start + width]
                                    if part == own:
                                        seen = key_pos[part][:, start : start + width] <= seen_to
                                        column = jnp.where(seen, column, mask_floor)
                                    columns.append(column)
                            top = jnp.max(
                                functools.reduce(jnp.maximum, columns), axis=-1, keepdims=True
                            )
                            top = jnp.broadcast_to(top, (R, D))
                            if not first:
                                before = max_ref[piece, head, yy, block]
                                top = jnp.maximum(top, before)
                                factors.append(jnp.exp2((before - top) * scaling))
                            weights = [jnp.exp2((s - top[:, :width]) * scaling) for s in columns]
                            total = sum(weights)
                            if width < D:
                                filler = jnp.zeros((R, D - width), total.dtype)
                                total = jnp.concatenate([total, filler], axis=1)
                            if not first:
                                total = total + sum_ref[piece, head, yy, block] * factors[-1]
                            totals.append(total)
                            rounded.append([w.astype(jnp.bfloat16) for w in weights])
                            if not last:
                                max_ref[piece, head, yy, block] = top
                        weights = [jnp.concatenate(ws, axis=0) for ws in zip(*rounded)]
                        if width == D:
                            weights = [jnp.concatenate(weights, axis=1)]
                        total = jnp.concatenate(totals, axis=0)
                        shared = units(1, head, early if own == "early" else early + late)
                        update, start = 0.0, 0
                        for w in weights:
                            update = update + jnp.dot(
                                w,
                                shared[start : start + w.shape[1]],
                                preferred_element_type=jnp.float32,
                            )
                            start += w.shape[1]
                        if not first:
                            factor = jnp.concatenate(factors, axis=0)
                            update = update + acc_ref[piece, head, yy] * factor
                    else:
                        total, update = sum_ref[piece, head, yy], acc_ref[piece, head, yy]
                    if last:
                        mixed = update * (1.0 / jnp.sum(total, axis=-1, keepdims=True))
                        out_part[piece, yy, :, head] = mixed.astype(jnp.bfloat16).reshape(
                            C, G, R, D
                        )
                    else:
                        sum_ref[piece, head, yy] = total
                        acc_ref[piece, head, yy] = update
                if last:
                    for dc in range(1, C):
                        o_copy(dy, dc, piece).start()

                    def keep():
                        out_ref[y * C + c, :, :, pl.ds(piece * R, R)] = out_part[piece, y, c]

                    pl.when(dy > 0)(lambda: o_copy(dy, 0, piece).start())
                    pl.when(dy == 0)(keep)
            return unused

        lax.fori_loop(0, Y, blocks_of, 0)

    def o_copy(dy, dc, piece):
        xx, yy, cc = member(0, dy, dc)
        return remote(
            out_part.at[piece, yy, cc],
            out_ref.at[y * C + c, :, :, pl.ds(piece * R, R)],
            o_send.at[dy, dc, piece],
            o_recv.at[dy, dc, piece],
            device(x, cc, z * Y + yy),
        )

    if whole_way > 0:
        receive(1)
    for offset in offsets:
        q_copy(*offset).wait_recv()
    attend([z] + [below(1), above(1)] * min(1, whole_way), True, Z == 1)

    def later(d):
        receive(d)
        attend([below(d), above(d)], False, False)

    small_loop(2, whole_way + 1, later)
    if Z % 2 == 0:
        opposite = above(Z // 2)
        for j, unit in enumerate(units_here):
            z_copy(opposite, 1 - j % 2, unit).wait_recv()
        attend([opposite], False, True)
    elif Z > 1:
        attend([], False, True)

    for offset in offsets:
        kv_copy(*offset).wait_send()
        q_copy(*offset).wait_send()
    def sent(d):
        for j, unit in enumerate(units_here):
            z_copy(below(d), 1, unit).wait_send()
            z_copy(above(d), 0, unit).wait_send()

    small_loop(0, whole_way, sent)
    if Z % 2 == 0:
        for j, unit in enumerate(units_here):
            if j % 2 == 0:
                z_copy(below(Z // 2 - 1), 1, unit).wait_send()
            else:
                z_copy(above(Z // 2 - 1), 0, unit).wait_send()
    for dx, dy, dc in offsets:
        if dx == 0:
            for piece in range(X):
                o_copy(dy, dc, piece).wait()


def per_device(queries, keys, values, run_index):
    X, C, B = lax.axis_size("heads"), lax.axis_size("team"), lax.axis_size("blk")
    R, QH, D = queries.shape[1:]
    KVH = keys.shape[2]
    Y = math.gcd(KVH // (X * C), B)
    KVL = KVH // (X * C * Y)
    G = QH // KVH
    Z = B // Y
    freqs = inverse_freqs(D)
    freqs = jnp.asarray(np.concatenate([freqs, freqs])[None], jnp.float32)
    rows = C * G * R
    hbm = pl.BlockSpec(memory_space=pltpu.HBM)
    dma = pltpu.SemaphoreType.DMA
    bf16, f32 = jnp.bfloat16, jnp.float32
    out = pl.pallas_call(
        functools.partial(attend_kernel, (X, C, Z, Y, R, KVL, G, D)),
        out_shape=pltpu.VMEM((Y * C, KVL, G, X * R, D), bf16),
        in_specs=[hbm] * 5,
        out_specs=pl.BlockSpec(memory_space=pltpu.VMEM),
        scratch_shapes=[
            pltpu.SMEM(run_index.shape, run_index.dtype),
            pltpu.VMEM(freqs.shape, f32),
            pltpu.VMEM(queries.shape, bf16),
            pltpu.VMEM(keys.shape, bf16),
            pltpu.VMEM(values.shape, bf16),
            dma((5,)),
            pltpu.VMEM((X * Y * C, 2, KVL, R, D), bf16),
            pltpu.VMEM((X * Y * C, KVL, G, R, D), bf16),
            pltpu.VMEM((Z, X, Y, C, 2, KVL, R, D), bf16),
            pltpu.VMEM((X, KVL, Y, C, G, R, D), bf16),
            pltpu.VMEM((X, KVL, Y, rows, D), f32),
            pltpu.VMEM((X, KVL, Y, rows, D), f32),
            pltpu.VMEM((X, KVL, Y, rows, D), f32),
            pltpu.VMEM((X, Y, C, R, D), jnp.int32),
            pltpu.VMEM((X, Y, C, KVL, G, R, D), bf16),
            dma((X, Y, C)),
            dma((X, Y, C)),
            dma((X, Y, C)),
            dma((X, Y, C)),
            dma((2, Z, X, Y)),
            dma((Z, X, Y)),
            dma((Y, C, X)),
            dma((Y, C, X)),
        ],
        compiler_params=pltpu.CompilerParams(
            collective_id=0, has_side_effects=True, vmem_limit_bytes=60 * 2**20
        ),
    )(run_index, freqs, queries, keys, values)
    return jnp.transpose(out.reshape(Y * C * KVL * G, X * R, D), (1, 0, 2))


def solution(mesh):
    in_specs = (
        P("heads", ("team", "blk"), None, None),
        P("heads", ("team", "blk"), None, None),
        P("heads", ("team", "blk"), None, None),
        P(),
    )
    out_specs = P(("team", "blk"), "heads", None)
    return jax.shard_map(
        per_device, mesh=mesh, in_specs=in_specs, out_specs=out_specs, check_vma=False
    )
```

```python
import functools
import math

import jax
import jax.numpy as jnp
import numpy as np
from jax import lax
from jax.experimental import pallas as pl
from jax.experimental.pallas import tpu as pltpu
from jax.sharding import PartitionSpec as P

mask_floor = -1e30
rope_theta = 500000.0
rope_factor = 8.0
low_factor = 1.0
high_factor = 4.0
initial_context = 8192.0


def inverse_freqs(head_width):
    counter = np.arange(head_width // 2, dtype=np.float64)
    base_freq = 1.0 / rope_theta ** (2.0 * counter / head_width)
    wavelength = 2.0 * np.pi / base_freq
    smooth = (initial_context / wavelength - low_factor) / (high_factor - low_factor)
    blended = (1.0 - smooth) * base_freq / rope_factor + smooth * base_freq
    middle = np.where(wavelength > initial_context / low_factor, base_freq / rope_factor, blended)
    return np.where(wavelength < initial_context / high_factor, base_freq, middle)


def small_loop(first, last, body):
    if last - first <= 4:
        for at in range(first, last):
            body(at)
    else:
        lax.fori_loop(first, last, lambda at, unused: (body(at), unused)[1], 0)


def attend_kernel(
    dims,
    run_hbm,
    freq_hbm,
    q_hbm,
    k_hbm,
    v_hbm,
    out_ref,
    run_ref,
    freq_ref,
    q_ref,
    k_ref,
    v_ref,
    load_sem,
    kv_out,
    q_out,
    kv_all,
    q_all,
    acc_ref,
    max_ref,
    sum_ref,
    pos_ref,
    out_part,
    kv_send,
    kv_recv,
    q_send,
    q_recv,
    z_send,
    z_recv,
    o_send,
    o_recv,
):
    X, C, Z, Y, R, KVL, G, D = dims
    S = C * Z * Y
    half = X * R // 2
    rows = C * G * R
    x, c, b = lax.axis_index("heads"), lax.axis_index("team"), lax.axis_index("blk")
    z, y = b // Y, b % Y
    mine = (x * Y + y) * C + c
    def device(xx, cc, bb):
        return {"heads": xx, "team": cc, "blk": bb}

    loads = [
        pltpu.make_async_copy(src, dst, load_sem.at[at])
        for at, (src, dst) in enumerate(
            [(run_hbm, run_ref), (freq_hbm, freq_ref), (k_hbm, k_ref), (v_hbm, v_ref), (q_hbm, q_ref)]
        )
    ]
    for load in loads:
        load.start()

    whole_way = (Z - 1) // 2
    up, down = (z + 1) % Z, (z + Z - 1) % Z

    def below(d):
        return (z + Z - d) % Z

    def above(d):
        return (z + d) % Z

    offsets = [
        (dx, dy, dc)
        for dx in range(X)
        for dy in range(Y)
        for dc in range(C)
        if (dx, dy, dc) != (0, 0, 0)
    ]

    barrier = pltpu.get_barrier_semaphore()

    def greet(xx, cc, bb):
        pl.semaphore_signal(
            barrier, inc=1, device_id=device(xx, cc, bb), device_id_type=pl.DeviceIdType.MESH
        )

    def member(dx, dy, dc):
        return (x + dx) % X, (y + dy) % Y, (c + dc) % C

    for offset in offsets:
        xx, yy, cc = member(*offset)
        greet(xx, cc, z * Y + yy)
    if Z > 1:
        greet(x, c, up * Y + y)
        greet(x, c, down * Y + y)

    def first_pos(slot, piece):
        run = run_ref[slot]
        start = piece * R
        if isinstance(piece, int):
            return run * half + start if start < half else (2 * S - 1 - run) * half + start - half
        return jnp.where(start < half, run * half, (2 * S - 1 - run) * half - half) + start

    loads[0].wait()
    loads[1].wait()

    own_first = first_pos(c * (Z * Y) + b, x)
    pos = own_first + lax.broadcasted_iota(jnp.int32, (R, D), 0)
    angles = pos.astype(jnp.float32) * freq_ref[...]
    cosine = jnp.cos(angles)
    sine = jnp.sin(angles)
    lanes = lax.broadcasted_iota(jnp.int32, (R, D), 1)
    sine = jnp.where(lanes < D // 2, -sine, sine)

    def by_head(ref, first, count):
        return jnp.swapaxes(ref[0, :, first : first + count, :].astype(jnp.float32), 0, 1)

    def rotated(values):
        turned = pltpu.roll(values, D // 2, 2)
        return values * cosine[None] + turned * sine[None]

    loads[2].wait()
    loads[3].wait()
    kv_heads = X * Y * C * KVL
    kv_out[:, 0] = (
        rotated(by_head(k_ref, 0, kv_heads)).astype(jnp.bfloat16).reshape(X * Y * C, KVL, R, D)
    )
    kv_out[:, 1] = by_head(v_ref, 0, kv_heads).astype(jnp.bfloat16).reshape(X * Y * C, KVL, R, D)
    kv_all[z, x, y, c] = kv_out[mine]

    pl.semaphore_wait(barrier, len(offsets) + (2 if Z > 1 else 0))

    def remote(src, dst, send, recv, to):
        return pltpu.make_async_remote_copy(
            src_ref=src,
            dst_ref=dst,
            send_sem=send,
            recv_sem=recv,
            device_id=to,
            device_id_type=pl.DeviceIdType.MESH,
        )

    units_here = [((x + X - dx) % X, (y + Y - dy) % Y) for dx in range(X) for dy in range(Y)]
    units_sorted = [(piece, (y + Y - dy) % Y) for piece in range(X) for dy in range(Y)]

    def z_copy(at, upward, unit):
        return remote(
            kv_all.at[at, *unit],
            kv_all.at[at, *unit],
            z_send.at[upward, at, *unit],
            z_recv.at[at, *unit],
            device(x, c, (up if upward else down) * Y + y),
        )

    def goes(d, upward, j):
        return d <= whole_way or (2 * d == Z and j % 2 == 1 - upward)

    def pass_on(at, d, upward, j, unit):
        if isinstance(d, int):
            if goes(d, upward, j):
                z_copy(at, upward, unit).start()
        else:
            here = (d <= whole_way) | ((2 * d == Z) & (j % 2 == 1 - upward))
            pl.when(here)(lambda: z_copy(at, upward, unit).start())

    def kv_copy(*offset):
        xx, yy, cc = member(*offset)
        return remote(
            kv_out.at[(xx * Y + yy) * C + cc],
            kv_all.at[z, x, y, c],
            kv_send.at[*offset],
            kv_recv.at[*offset],
            device(xx, cc, z * Y + yy),
        )

    def q_copy(*offset):
        xx, yy, cc = member(*offset)
        return remote(
            q_out.at[(xx * Y + yy) * C + cc],
            q_all.at[x, :, y, c],
            q_send.at[*offset],
            q_recv.at[*offset],
            device(xx, cc, z * Y + yy),
        )

    for offset in offsets:
        kv_copy(*offset).start()

    loads[4].wait()
    q_heads = KVL * G
    share = math.gcd(X * Y * C, max(1, 8 // q_heads))
    for to in range(0, X * Y * C, share):
        q_out[to : to + share] = (
            rotated(by_head(q_ref, to * q_heads, share * q_heads))
            .astype(jnp.bfloat16)
            .reshape(share, KVL, G, R, D)
        )
    q_all[x, :, y, c] = q_out[mine]
    for offset in offsets:
        q_copy(*offset).start()
    for dx in range(X):
        for dy in range(Y):
            for dc in range(C):
                if (dx, dy, dc) != (0, 0, 0):
                    kv_copy(dx, dy, dc).wait_recv()
            pass_on(z, 1, 1, dx * Y + dy, units_here[dx * Y + dy])
            pass_on(z, 1, 0, dx * Y + dy, units_here[dx * Y + dy])

    def receive(d):
        for j, unit in enumerate(units_sorted):
            z_copy(below(d), 1, unit).wait_recv()
            pass_on(below(d), d + 1, 1, j, unit)
            z_copy(above(d), 0, unit).wait_recv()
            pass_on(above(d), d + 1, 0, j, unit)

    scaling = math.log2(math.e) * D ** (-0.5)

    def key_positions(planes, pieces):
        count = len(pieces) * len(planes) * Y * C * R
        lane = lax.broadcasted_iota(jnp.int32, (1, count), 1)
        segment = lane // R
        total = lane % R
        at = 0
        for piece in pieces:
            for plane in planes:
                for yy in range(Y):
                    for cc in range(C):
                        slot = cc * (Z * Y) + plane * Y + yy
                        total = total + jnp.where(segment == at, first_pos(slot, piece), 0)
                        at += 1
        return total

    def query_positions(piece, yy, cc):
        row = lax.broadcasted_iota(jnp.int32, (R, D), 0)
        return row + first_pos(cc * (Z * Y) + z * Y + yy, piece)

    for piece in range(X):
        for yy in range(Y):
            for cc in range(C):
                pos_ref[piece, yy, cc] = query_positions(piece, yy, cc)

    early = list(range(X // 2))
    late = list(range(X // 2, X))

    def attend(planes, pieces_here, first, last):

        def units(kind, head, pieces):
            return jnp.concatenate(
                [
                    kv_all[plane, p, yy, cc, kind, head]
                    for p in pieces
                    for plane in planes
                    for yy in range(Y)
                    for cc in range(C)
                ],
                axis=0,
            )

        if planes:
            key_pos = {"early": key_positions(planes, early), "late": key_positions(planes, late)}
        def blocks_of(step, unused):
            dy = Y - 1 - step
            yy = (y + dy) % Y
            for piece in pieces_here:
                own = "early" if piece in early else "late"
                parts = ["early"] if own == "early" else ["early", "late"]
                for head in range(KVL):
                    if planes:
                        query = q_all[piece, head, yy].reshape(rows, D)
                        scores = [
                            lax.dot_general(
                                query,
                                units(0, head, early if part == "early" else late),
                                (((1,), (1,)), ((), ())),
                                preferred_element_type=jnp.float32,
                            )
                            for part in parts
                        ]
                        width = math.gcd(scores[0].shape[1], D)
                        rounded, totals, factors = [], [], []
                        for at in range(0, rows, R):
                            block = slice(at, at + R)
                            seen_to = pos_ref[piece, yy, at // (G * R), :, :width]
                            columns = []
                            for part, s in zip(parts, scores):
                                for start in range(0, s.shape[1], width):
                                    column = s[block, start : start + width]
                                    if part == own:
                                        seen = key_pos[part][:, start : start + width] <= seen_to
                                        column = jnp.where(seen, column, mask_floor)
                                    columns.append(column)
                            top = jnp.max(
                                functools.reduce(jnp.maximum, columns), axis=-1, keepdims=True
                            )
                            top = jnp.broadcast_to(top, (R, D))
                            if not first:
                                before = max_ref[piece, head, yy, block]
                                top = jnp.maximum(top, before)
                                factors.append(jnp.exp2((before - top) * scaling))
                            weights = [jnp.exp2((s - top[:, :width]) * scaling) for s in columns]
                            total = sum(weights)
                            if width < D:
                                filler = jnp.zeros((R, D - width), total.dtype)
                                total = jnp.concatenate([total, filler], axis=1)
                            if not first:
                                total = total + sum_ref[piece, head, yy, block] * factors[-1]
                            totals.append(total)
                            rounded.append([w.astype(jnp.bfloat16) for w in weights])
                            if not last:
                                max_ref[piece, head, yy, block] = top
                        weights = [jnp.concatenate(ws, axis=0) for ws in zip(*rounded)]
                        if width == D:
                            weights = [jnp.concatenate(weights, axis=1)]
                        total = jnp.concatenate(totals, axis=0)
                        shared = units(1, head, early if own == "early" else early + late)
                        update, start = 0.0, 0
                        for w in weights:
                            update = update + jnp.dot(
                                w,
                                shared[start : start + w.shape[1]],
                                preferred_element_type=jnp.float32,
                            )
                            start += w.shape[1]
                        if not first:
                            factor = jnp.concatenate(factors, axis=0)
                            update = update + acc_ref[piece, head, yy] * factor
                    else:
                        total, update = sum_ref[piece, head, yy], acc_ref[piece, head, yy]
                    if last:
                        mixed = update * (1.0 / jnp.sum(total, axis=-1, keepdims=True))
                        out_part[piece, yy, :, head] = mixed.astype(jnp.bfloat16).reshape(
                            C, G, R, D
                        )
                    else:
                        sum_ref[piece, head, yy] = total
                        acc_ref[piece, head, yy] = update
                if last:
                    for dc in range(1, C):
                        o_copy(dy, dc, piece).start()

                    def keep():
                        out_ref[y * C + c, :, :, pl.ds(piece * R, R)] = out_part[piece, y, c]

                    pl.when(dy > 0)(lambda: o_copy(dy, 0, piece).start())
                    pl.when(dy == 0)(keep)
            return unused

        lax.fori_loop(0, Y, blocks_of, 0)

    def o_copy(dy, dc, piece):
        xx, yy, cc = member(0, dy, dc)
        return remote(
            out_part.at[piece, yy, cc],
            out_ref.at[y * C + c, :, :, pl.ds(piece * R, R)],
            o_send.at[dy, dc, piece],
            o_recv.at[dy, dc, piece],
            device(x, cc, z * Y + yy),
        )

    if whole_way > 0:
        receive(1)
    for offset in offsets:
        q_copy(*offset).wait_recv()
    attend([z] + [below(1), above(1)] * min(1, whole_way), range(X), True, Z == 1)

    def later(d):
        receive(d)
        attend([below(d), above(d)], range(X), False, False)

    small_loop(2, whole_way + 1, later)
    if Z % 2 == 0:
        opposite = above(Z // 2)
        for pieces in (early, late):
            for j, unit in enumerate(units_sorted):
                if j // Y in pieces:
                    z_copy(opposite, 1 - j % 2, unit).wait_recv()
            attend([opposite], pieces, False, True)
    elif Z > 1:
        attend([], range(X), False, True)

    for offset in offsets:
        kv_copy(*offset).wait_send()
        q_copy(*offset).wait_send()
    def sent(d):
        for j, unit in enumerate(units_sorted):
            z_copy(below(d), 1, unit).wait_send()
            z_copy(above(d), 0, unit).wait_send()

    small_loop(0, whole_way, sent)
    if Z % 2 == 0:
        for j, unit in enumerate(units_sorted):
            if j % 2 == 0:
                z_copy(below(Z // 2 - 1), 1, unit).wait_send()
            else:
                z_copy(above(Z // 2 - 1), 0, unit).wait_send()
    for dx, dy, dc in offsets:
        if dx == 0:
            for piece in range(X):
                o_copy(dy, dc, piece).wait()


def per_device(queries, keys, values, run_index):
    X, C, B = lax.axis_size("heads"), lax.axis_size("team"), lax.axis_size("blk")
    R, QH, D = queries.shape[1:]
    KVH = keys.shape[2]
    Y = math.gcd(KVH // (X * C), B)
    KVL = KVH // (X * C * Y)
    G = QH // KVH
    Z = B // Y
    freqs = inverse_freqs(D)
    freqs = jnp.asarray(np.concatenate([freqs, freqs])[None], jnp.float32)
    rows = C * G * R
    hbm = pl.BlockSpec(memory_space=pltpu.HBM)
    dma = pltpu.SemaphoreType.DMA
    bf16, f32 = jnp.bfloat16, jnp.float32
    out = pl.pallas_call(
        functools.partial(attend_kernel, (X, C, Z, Y, R, KVL, G, D)),
        out_shape=pltpu.VMEM((Y * C, KVL, G, X * R, D), bf16),
        in_specs=[hbm] * 5,
        out_specs=pl.BlockSpec(memory_space=pltpu.VMEM),
        scratch_shapes=[
            pltpu.SMEM(run_index.shape, run_index.dtype),
            pltpu.VMEM(freqs.shape, f32),
            pltpu.VMEM(queries.shape, bf16),
            pltpu.VMEM(keys.shape, bf16),
            pltpu.VMEM(values.shape, bf16),
            dma((5,)),
            pltpu.VMEM((X * Y * C, 2, KVL, R, D), bf16),
            pltpu.VMEM((X * Y * C, KVL, G, R, D), bf16),
            pltpu.VMEM((Z, X, Y, C, 2, KVL, R, D), bf16),
            pltpu.VMEM((X, KVL, Y, C, G, R, D), bf16),
            pltpu.VMEM((X, KVL, Y, rows, D), f32),
            pltpu.VMEM((X, KVL, Y, rows, D), f32),
            pltpu.VMEM((X, KVL, Y, rows, D), f32),
            pltpu.VMEM((X, Y, C, R, D), jnp.int32),
            pltpu.VMEM((X, Y, C, KVL, G, R, D), bf16),
            dma((X, Y, C)),
            dma((X, Y, C)),
            dma((X, Y, C)),
            dma((X, Y, C)),
            dma((2, Z, X, Y)),
            dma((Z, X, Y)),
            dma((Y, C, X)),
            dma((Y, C, X)),
        ],
        compiler_params=pltpu.CompilerParams(
            collective_id=0, has_side_effects=True, vmem_limit_bytes=60 * 2**20
        ),
    )(run_index, freqs, queries, keys, values)
    return jnp.transpose(out.reshape(Y * C * KVL * G, X * R, D), (1, 0, 2))


def solution(mesh):
    in_specs = (
        P("heads", ("team", "blk"), None, None),
        P("heads", ("team", "blk"), None, None),
        P("heads", ("team", "blk"), None, None),
        P(),
    )
    out_specs = P(("team", "blk"), "heads", None)
    return jax.shard_map(
        per_device, mesh=mesh, in_specs=in_specs, out_specs=out_specs, check_vma=False
    )
```

```python
import functools
import math

import jax
import jax.numpy as jnp
import numpy as np
from jax import lax
from jax.experimental import pallas as pl
from jax.experimental.pallas import tpu as pltpu
from jax.sharding import PartitionSpec as P

mask_floor = -1e30
rope_theta = 500000.0
rope_factor = 8.0
low_factor = 1.0
high_factor = 4.0
initial_context = 8192.0


def inverse_freqs(head_width):
    counter = np.arange(head_width // 2, dtype=np.float64)
    base_freq = 1.0 / rope_theta ** (2.0 * counter / head_width)
    wavelength = 2.0 * np.pi / base_freq
    smooth = (initial_context / wavelength - low_factor) / (high_factor - low_factor)
    blended = (1.0 - smooth) * base_freq / rope_factor + smooth * base_freq
    middle = np.where(wavelength > initial_context / low_factor, base_freq / rope_factor, blended)
    return np.where(wavelength < initial_context / high_factor, base_freq, middle)


def small_loop(first, last, body):
    if last - first <= 4:
        for at in range(first, last):
            body(at)
    else:
        lax.fori_loop(first, last, lambda at, unused: (body(at), unused)[1], 0)


def attend_kernel(
    dims,
    run_hbm,
    freq_hbm,
    q_hbm,
    k_hbm,
    v_hbm,
    out_ref,
    run_ref,
    freq_ref,
    q_ref,
    k_ref,
    v_ref,
    load_sem,
    kv_out,
    q_out,
    kv_all,
    q_all,
    acc_ref,
    max_ref,
    sum_ref,
    pos_ref,
    out_part,
    kv_send,
    kv_recv,
    q_send,
    q_recv,
    z_send,
    z_recv,
    o_send,
    o_recv,
):
    X, C, Z, Y, R, KVL, G, D = dims
    S = C * Z * Y
    half = X * R // 2
    rows = C * G * R
    x, c, b = lax.axis_index("heads"), lax.axis_index("team"), lax.axis_index("blk")
    z, y = b // Y, b % Y
    mine = (x * Y + y) * C + c
    def device(xx, cc, bb):
        return {"heads": xx, "team": cc, "blk": bb}

    loads = [
        pltpu.make_async_copy(src, dst, load_sem.at[at])
        for at, (src, dst) in enumerate(
            [(run_hbm, run_ref), (freq_hbm, freq_ref), (k_hbm, k_ref), (v_hbm, v_ref), (q_hbm, q_ref)]
        )
    ]
    for load in loads:
        load.start()

    whole_way = (Z - 1) // 2
    up, down = (z + 1) % Z, (z + Z - 1) % Z

    def below(d):
        return (z + Z - d) % Z

    def above(d):
        return (z + d) % Z

    offsets = [
        (dx, dy, dc)
        for dx in range(X)
        for dy in range(Y)
        for dc in range(C)
        if (dx, dy, dc) != (0, 0, 0)
    ]

    barrier = pltpu.get_barrier_semaphore()

    def greet(xx, cc, bb):
        pl.semaphore_signal(
            barrier, inc=1, device_id=device(xx, cc, bb), device_id_type=pl.DeviceIdType.MESH
        )

    def member(dx, dy, dc):
        return (x + dx) % X, (y + dy) % Y, (c + dc) % C

    for offset in offsets:
        xx, yy, cc = member(*offset)
        greet(xx, cc, z * Y + yy)
    if Z > 1:
        greet(x, c, up * Y + y)
        greet(x, c, down * Y + y)

    def first_pos(slot, piece):
        run = run_ref[slot]
        start = piece * R
        if isinstance(piece, int):
            return run * half + start if start < half else (2 * S - 1 - run) * half + start - half
        return jnp.where(start < half, run * half, (2 * S - 1 - run) * half - half) + start

    loads[0].wait()
    loads[1].wait()

    own_first = first_pos(c * (Z * Y) + b, x)
    pos = own_first + lax.broadcasted_iota(jnp.int32, (R, D), 0)
    angles = pos.astype(jnp.float32) * freq_ref[...]
    cosine = jnp.cos(angles)
    sine = jnp.sin(angles)
    lanes = lax.broadcasted_iota(jnp.int32, (R, D), 1)
    sine = jnp.where(lanes < D // 2, -sine, sine)

    def by_head(ref, first, count):
        return jnp.swapaxes(ref[0, :, first : first + count, :].astype(jnp.float32), 0, 1)

    def rotated(values):
        turned = pltpu.roll(values, D // 2, 2)
        return values * cosine[None] + turned * sine[None]

    loads[2].wait()
    loads[3].wait()
    kv_heads = X * Y * C * KVL
    kv_out[:, 0] = (
        rotated(by_head(k_ref, 0, kv_heads)).astype(jnp.bfloat16).reshape(X * Y * C, KVL, R, D)
    )
    kv_out[:, 1] = by_head(v_ref, 0, kv_heads).astype(jnp.bfloat16).reshape(X * Y * C, KVL, R, D)
    kv_all[z, x, y, c] = kv_out[mine]

    pl.semaphore_wait(barrier, len(offsets) + (2 if Z > 1 else 0))

    def remote(src, dst, send, recv, to):
        return pltpu.make_async_remote_copy(
            src_ref=src,
            dst_ref=dst,
            send_sem=send,
            recv_sem=recv,
            device_id=to,
            device_id_type=pl.DeviceIdType.MESH,
        )

    units_here = [((x + X - dx) % X, (y + Y - dy) % Y) for dx in range(X) for dy in range(Y)]
    units_sorted = [(piece, (y + Y - dy) % Y) for piece in range(X) for dy in range(Y)]

    def z_copy(at, upward, unit):
        return remote(
            kv_all.at[at, *unit],
            kv_all.at[at, *unit],
            z_send.at[upward, at, *unit],
            z_recv.at[at, *unit],
            device(x, c, (up if upward else down) * Y + y),
        )

    def pass_on(at, d, upward, unit):
        relays = (d <= whole_way) | ((2 * d == Z) & (z % 2 == 1 - upward))
        if isinstance(d, int) and d <= whole_way:
            z_copy(at, upward, unit).start()
        else:
            pl.when(relays)(lambda: z_copy(at, upward, unit).start())

    def kv_copy(*offset):
        xx, yy, cc = member(*offset)
        return remote(
            kv_out.at[(xx * Y + yy) * C + cc],
            kv_all.at[z, x, y, c],
            kv_send.at[*offset],
            kv_recv.at[*offset],
            device(xx, cc, z * Y + yy),
        )

    def q_copy(*offset):
        xx, yy, cc = member(*offset)
        return remote(
            q_out.at[(xx * Y + yy) * C + cc],
            q_all.at[x, :, y, c],
            q_send.at[*offset],
            q_recv.at[*offset],
            device(xx, cc, z * Y + yy),
        )

    for offset in offsets:
        kv_copy(*offset).start()

    loads[4].wait()
    q_heads = KVL * G
    share = math.gcd(X * Y * C, max(1, 8 // q_heads))
    for to in range(0, X * Y * C, share):
        q_out[to : to + share] = (
            rotated(by_head(q_ref, to * q_heads, share * q_heads))
            .astype(jnp.bfloat16)
            .reshape(share, KVL, G, R, D)
        )
    q_all[x, :, y, c] = q_out[mine]
    for offset in offsets:
        q_copy(*offset).start()
    for dx in range(X):
        for dy in range(Y):
            for dc in range(C):
                if (dx, dy, dc) != (0, 0, 0):
                    kv_copy(dx, dy, dc).wait_recv()
            pass_on(z, 1, 1, units_here[dx * Y + dy])
            pass_on(z, 1, 0, units_here[dx * Y + dy])

    def receive(d):
        for unit in units_sorted:
            z_copy(below(d), 1, unit).wait_recv()
            pass_on(below(d), d + 1, 1, unit)
            z_copy(above(d), 0, unit).wait_recv()
            pass_on(above(d), d + 1, 0, unit)

    scaling = math.log2(math.e) * D ** (-0.5)

    def key_positions(planes, pieces):
        count = len(pieces) * len(planes) * Y * C * R
        lane = lax.broadcasted_iota(jnp.int32, (1, count), 1)
        segment = lane // R
        total = lane % R
        at = 0
        for piece in pieces:
            for plane in planes:
                for yy in range(Y):
                    for cc in range(C):
                        slot = cc * (Z * Y) + plane * Y + yy
                        total = total + jnp.where(segment == at, first_pos(slot, piece), 0)
                        at += 1
        return total

    def query_positions(piece, yy, cc):
        row = lax.broadcasted_iota(jnp.int32, (R, D), 0)
        return row + first_pos(cc * (Z * Y) + z * Y + yy, piece)

    for piece in range(X):
        for yy in range(Y):
            for cc in range(C):
                pos_ref[piece, yy, cc] = query_positions(piece, yy, cc)

    early = list(range(X // 2))
    late = list(range(X // 2, X))

    def attend(planes, pieces_here, first, last):

        def units(kind, head, pieces):
            return jnp.concatenate(
                [
                    kv_all[plane, p, yy, cc, kind, head]
                    for p in pieces
                    for plane in planes
                    for yy in range(Y)
                    for cc in range(C)
                ],
                axis=0,
            )

        if planes:
            key_pos = {"early": key_positions(planes, early), "late": key_positions(planes, late)}
        def blocks_of(step, unused):
            dy = Y - 1 - step
            yy = (y + dy) % Y
            for piece in pieces_here:
                own = "early" if piece in early else "late"
                parts = ["early"] if own == "early" else ["early", "late"]
                for head in range(KVL):
                    if planes:
                        query = q_all[piece, head, yy].reshape(rows, D)
                        scores = [
                            lax.dot_general(
                                query,
                                units(0, head, early if part == "early" else late),
                                (((1,), (1,)), ((), ())),
                                preferred_element_type=jnp.float32,
                            )
                            for part in parts
                        ]
                        width = math.gcd(scores[0].shape[1], D)
                        rounded, totals, factors = [], [], []
                        for at in range(0, rows, R):
                            block = slice(at, at + R)
                            seen_to = pos_ref[piece, yy, at // (G * R), :, :width]
                            columns = []
                            for part, s in zip(parts, scores):
                                for start in range(0, s.shape[1], width):
                                    column = s[block, start : start + width]
                                    if part == own:
                                        seen = key_pos[part][:, start : start + width] <= seen_to
                                        column = jnp.where(seen, column, mask_floor)
                                    columns.append(column)
                            top = jnp.max(
                                functools.reduce(jnp.maximum, columns), axis=-1, keepdims=True
                            )
                            top = jnp.broadcast_to(top, (R, D))
                            if not first:
                                before = max_ref[piece, head, yy, block]
                                top = jnp.maximum(top, before)
                                factors.append(jnp.exp2((before - top) * scaling))
                            weights = [jnp.exp2((s - top[:, :width]) * scaling) for s in columns]
                            total = sum(weights)
                            if width < D:
                                filler = jnp.zeros((R, D - width), total.dtype)
                                total = jnp.concatenate([total, filler], axis=1)
                            if not first:
                                total = total + sum_ref[piece, head, yy, block] * factors[-1]
                            totals.append(total)
                            rounded.append([w.astype(jnp.bfloat16) for w in weights])
                            if not last:
                                max_ref[piece, head, yy, block] = top
                        weights = [jnp.concatenate(ws, axis=0) for ws in zip(*rounded)]
                        if width == D:
                            weights = [jnp.concatenate(weights, axis=1)]
                        total = jnp.concatenate(totals, axis=0)
                        shared = units(1, head, early if own == "early" else early + late)
                        update, start = 0.0, 0
                        for w in weights:
                            update = update + jnp.dot(
                                w,
                                shared[start : start + w.shape[1]],
                                preferred_element_type=jnp.float32,
                            )
                            start += w.shape[1]
                        if not first:
                            factor = jnp.concatenate(factors, axis=0)
                            update = update + acc_ref[piece, head, yy] * factor
                    else:
                        total, update = sum_ref[piece, head, yy], acc_ref[piece, head, yy]
                    if last:
                        mixed = update * (1.0 / jnp.sum(total, axis=-1, keepdims=True))
                        out_part[piece, yy, :, head] = mixed.astype(jnp.bfloat16).reshape(
                            C, G, R, D
                        )
                    else:
                        sum_ref[piece, head, yy] = total
                        acc_ref[piece, head, yy] = update
                if last:
                    for dc in range(1, C):
                        o_copy(dy, dc, piece).start()

                    def keep():
                        out_ref[y * C + c, :, :, pl.ds(piece * R, R)] = out_part[piece, y, c]

                    pl.when(dy > 0)(lambda: o_copy(dy, 0, piece).start())
                    pl.when(dy == 0)(keep)
            return unused

        lax.fori_loop(0, Y, blocks_of, 0)

    def o_copy(dy, dc, piece):
        xx, yy, cc = member(0, dy, dc)
        return remote(
            out_part.at[piece, yy, cc],
            out_ref.at[y * C + c, :, :, pl.ds(piece * R, R)],
            o_send.at[dy, dc, piece],
            o_recv.at[dy, dc, piece],
            device(x, cc, z * Y + yy),
        )

    if whole_way > 0:
        receive(1)
    for offset in offsets:
        q_copy(*offset).wait_recv()
    attend([z] + [below(1), above(1)] * min(1, whole_way), range(X), True, Z == 1)

    def later(d):
        receive(d)
        attend([below(d), above(d)], range(X), False, False)

    small_loop(2, whole_way + 1, later)
    if Z % 2 == 0:
        opposite = above(Z // 2)
        for pieces in (early, late):
            for j, unit in enumerate(units_sorted):
                if j // Y in pieces:
                    z_copy(opposite, 1, unit).wait_recv()
            attend([opposite], pieces, False, True)
    elif Z > 1:
        attend([], range(X), False, True)

    for offset in offsets:
        kv_copy(*offset).wait_send()
        q_copy(*offset).wait_send()
    def sent(d):
        for j, unit in enumerate(units_sorted):
            z_copy(below(d), 1, unit).wait_send()
            z_copy(above(d), 0, unit).wait_send()

    small_loop(0, whole_way, sent)
    if Z % 2 == 0:
        for j, unit in enumerate(units_sorted):
            pl.when(z % 2 == 0)(lambda: z_copy(below(Z // 2 - 1), 1, unit).wait_send())
            pl.when(z % 2 == 1)(lambda: z_copy(above(Z // 2 - 1), 0, unit).wait_send())
    for dx, dy, dc in offsets:
        if dx == 0:
            for piece in range(X):
                o_copy(dy, dc, piece).wait()


def per_device(queries, keys, values, run_index):
    X, C, B = lax.axis_size("heads"), lax.axis_size("team"), lax.axis_size("blk")
    R, QH, D = queries.shape[1:]
    KVH = keys.shape[2]
    Y = math.gcd(KVH // (X * C), B)
    KVL = KVH // (X * C * Y)
    G = QH // KVH
    Z = B // Y
    freqs = inverse_freqs(D)
    freqs = jnp.asarray(np.concatenate([freqs, freqs])[None], jnp.float32)
    rows = C * G * R
    hbm = pl.BlockSpec(memory_space=pltpu.HBM)
    dma = pltpu.SemaphoreType.DMA
    bf16, f32 = jnp.bfloat16, jnp.float32
    out = pl.pallas_call(
        functools.partial(attend_kernel, (X, C, Z, Y, R, KVL, G, D)),
        out_shape=pltpu.VMEM((Y * C, KVL, G, X * R, D), bf16),
        in_specs=[hbm] * 5,
        out_specs=pl.BlockSpec(memory_space=pltpu.VMEM),
        scratch_shapes=[
            pltpu.SMEM(run_index.shape, run_index.dtype),
            pltpu.VMEM(freqs.shape, f32),
            pltpu.VMEM(queries.shape, bf16),
            pltpu.VMEM(keys.shape, bf16),
            pltpu.VMEM(values.shape, bf16),
            dma((5,)),
            pltpu.VMEM((X * Y * C, 2, KVL, R, D), bf16),
            pltpu.VMEM((X * Y * C, KVL, G, R, D), bf16),
            pltpu.VMEM((Z, X, Y, C, 2, KVL, R, D), bf16),
            pltpu.VMEM((X, KVL, Y, C, G, R, D), bf16),
            pltpu.VMEM((X, KVL, Y, rows, D), f32),
            pltpu.VMEM((X, KVL, Y, rows, D), f32),
            pltpu.VMEM((X, KVL, Y, rows, D), f32),
            pltpu.VMEM((X, Y, C, R, D), jnp.int32),
            pltpu.VMEM((X, Y, C, KVL, G, R, D), bf16),
            dma((X, Y, C)),
            dma((X, Y, C)),
            dma((X, Y, C)),
            dma((X, Y, C)),
            dma((2, Z, X, Y)),
            dma((Z, X, Y)),
            dma((Y, C, X)),
            dma((Y, C, X)),
        ],
        compiler_params=pltpu.CompilerParams(
            collective_id=0, has_side_effects=True, vmem_limit_bytes=60 * 2**20
        ),
    )(run_index, freqs, queries, keys, values)
    return jnp.transpose(out.reshape(Y * C * KVL * G, X * R, D), (1, 0, 2))


def solution(mesh):
    in_specs = (
        P("heads", ("team", "blk"), None, None),
        P("heads", ("team", "blk"), None, None),
        P("heads", ("team", "blk"), None, None),
        P(),
    )
    out_specs = P(("team", "blk"), "heads", None)
    return jax.shard_map(
        per_device, mesh=mesh, in_specs=in_specs, out_specs=out_specs, check_vma=False
    )
```

```python
import functools
import math

import jax
import jax.numpy as jnp
import numpy as np
from jax import lax
from jax.experimental import pallas as pl
from jax.experimental.pallas import tpu as pltpu
from jax.sharding import PartitionSpec as P

mask_floor = -1e30
rope_theta = 500000.0
rope_factor = 8.0
low_factor = 1.0
high_factor = 4.0
initial_context = 8192.0


def inverse_freqs(head_width):
    counter = np.arange(head_width // 2, dtype=np.float64)
    base_freq = 1.0 / rope_theta ** (2.0 * counter / head_width)
    wavelength = 2.0 * np.pi / base_freq
    smooth = (initial_context / wavelength - low_factor) / (high_factor - low_factor)
    blended = (1.0 - smooth) * base_freq / rope_factor + smooth * base_freq
    middle = np.where(wavelength > initial_context / low_factor, base_freq / rope_factor, blended)
    return np.where(wavelength < initial_context / high_factor, base_freq, middle)


def small_loop(first, last, body):
    if last - first <= 4:
        for at in range(first, last):
            body(at)
    else:
        lax.fori_loop(first, last, lambda at, unused: (body(at), unused)[1], 0)


def attend_kernel(
    dims,
    run_hbm,
    freq_hbm,
    q_hbm,
    k_hbm,
    v_hbm,
    out_ref,
    run_ref,
    freq_ref,
    q_ref,
    k_ref,
    v_ref,
    load_sem,
    kv_out,
    q_out,
    kv_all,
    q_all,
    acc_ref,
    max_ref,
    sum_ref,
    pos_ref,
    out_part,
    kv_send,
    kv_recv,
    q_send,
    q_recv,
    z_send,
    z_recv,
    o_send,
    o_recv,
):
    X, C, Z, Y, R, KVL, G, D = dims
    S = C * Z * Y
    half = X * R // 2
    rows = C * G * R
    x, c, b = lax.axis_index("heads"), lax.axis_index("team"), lax.axis_index("blk")
    z, y = b // Y, b % Y
    mine = (x * Y + y) * C + c
    def device(xx, cc, bb):
        return {"heads": xx, "team": cc, "blk": bb}

    loads = [
        pltpu.make_async_copy(src, dst, load_sem.at[at])
        for at, (src, dst) in enumerate(
            [(run_hbm, run_ref), (freq_hbm, freq_ref), (k_hbm, k_ref), (v_hbm, v_ref), (q_hbm, q_ref)]
        )
    ]
    for load in loads:
        load.start()

    whole_way = (Z - 1) // 2
    up, down = (z + 1) % Z, (z + Z - 1) % Z

    def below(d):
        return (z + Z - d) % Z

    def above(d):
        return (z + d) % Z

    offsets = [
        (dx, dy, dc)
        for dx in range(X)
        for dy in range(Y)
        for dc in range(C)
        if (dx, dy, dc) != (0, 0, 0)
    ]

    barrier = pltpu.get_barrier_semaphore()

    def greet(xx, cc, bb):
        pl.semaphore_signal(
            barrier, inc=1, device_id=device(xx, cc, bb), device_id_type=pl.DeviceIdType.MESH
        )

    def member(dx, dy, dc):
        return (x + dx) % X, (y + dy) % Y, (c + dc) % C

    for offset in offsets:
        xx, yy, cc = member(*offset)
        greet(xx, cc, z * Y + yy)
    if Z > 1:
        greet(x, c, up * Y + y)
        greet(x, c, down * Y + y)

    def first_pos(slot, piece):
        run = run_ref[slot]
        start = piece * R
        if isinstance(piece, int):
            return run * half + start if start < half else (2 * S - 1 - run) * half + start - half
        return jnp.where(start < half, run * half, (2 * S - 1 - run) * half - half) + start

    loads[0].wait()
    loads[1].wait()

    own_first = first_pos(c * (Z * Y) + b, x)
    pos = own_first + lax.broadcasted_iota(jnp.int32, (R, D), 0)
    angles = pos.astype(jnp.float32) * freq_ref[...]
    cosine = jnp.cos(angles)
    sine = jnp.sin(angles)
    lanes = lax.broadcasted_iota(jnp.int32, (R, D), 1)
    sine = jnp.where(lanes < D // 2, -sine, sine)

    def by_head(ref, first, count):
        return jnp.swapaxes(ref[0, :, first : first + count, :].astype(jnp.float32), 0, 1)

    def rotated(values):
        turned = pltpu.roll(values, D // 2, 2)
        return values * cosine[None] + turned * sine[None]

    loads[2].wait()
    loads[3].wait()
    kv_heads = X * Y * C * KVL
    kv_out[:, 0] = (
        rotated(by_head(k_ref, 0, kv_heads)).astype(jnp.bfloat16).reshape(X * Y * C, KVL, R, D)
    )
    kv_out[:, 1] = by_head(v_ref, 0, kv_heads).astype(jnp.bfloat16).reshape(X * Y * C, KVL, R, D)
    kv_all[z, x, y, c] = kv_out[mine]

    pl.semaphore_wait(barrier, len(offsets) + (2 if Z > 1 else 0))

    def remote(src, dst, send, recv, to):
        return pltpu.make_async_remote_copy(
            src_ref=src,
            dst_ref=dst,
            send_sem=send,
            recv_sem=recv,
            device_id=to,
            device_id_type=pl.DeviceIdType.MESH,
        )

    units_here = [((x + X - dx) % X, (y + Y - dy) % Y) for dx in range(X) for dy in range(Y)]
    units_sorted = [(piece, (y + Y - dy) % Y) for piece in range(X) for dy in range(Y)]

    def z_copy(at, upward, unit):
        return remote(
            kv_all.at[at, *unit],
            kv_all.at[at, *unit],
            z_send.at[upward, at, *unit],
            z_recv.at[at, *unit],
            device(x, c, (up if upward else down) * Y + y),
        )

    def pass_on(at, d, upward, unit):
        relays = (d <= whole_way) | ((2 * d == Z) & (z % 2 == 1 - upward))
        if isinstance(d, int) and d <= whole_way:
            z_copy(at, upward, unit).start()
        else:
            pl.when(relays)(lambda: z_copy(at, upward, unit).start())

    def kv_copy(*offset):
        xx, yy, cc = member(*offset)
        return remote(
            kv_out.at[(xx * Y + yy) * C + cc],
            kv_all.at[z, x, y, c],
            kv_send.at[*offset],
            kv_recv.at[*offset],
            device(xx, cc, z * Y + yy),
        )

    def q_copy(*offset):
        xx, yy, cc = member(*offset)
        return remote(
            q_out.at[(xx * Y + yy) * C + cc],
            q_all.at[x, :, y, c],
            q_send.at[*offset],
            q_recv.at[*offset],
            device(xx, cc, z * Y + yy),
        )

    for offset in offsets:
        kv_copy(*offset).start()

    def forward(dx, dy):
        for dc in range(C):
            if (dx, dy, dc) != (0, 0, 0):
                kv_copy(dx, dy, dc).wait_recv()
        pass_on(z, 1, 1, units_here[dx * Y + dy])
        pass_on(z, 1, 0, units_here[dx * Y + dy])

    forward(0, 0)

    loads[4].wait()
    q_heads = KVL * G
    share = math.gcd(X * Y * C, max(1, 8 // q_heads))
    for to in range(0, X * Y * C, share):
        q_out[to : to + share] = (
            rotated(by_head(q_ref, to * q_heads, share * q_heads))
            .astype(jnp.bfloat16)
            .reshape(share, KVL, G, R, D)
        )
    q_all[x, :, y, c] = q_out[mine]
    for offset in offsets:
        q_copy(*offset).start()
    for dx in range(X):
        for dy in range(Y):
            if (dx, dy) != (0, 0):
                forward(dx, dy)

    def receive(d):
        for unit in units_sorted:
            z_copy(below(d), 1, unit).wait_recv()
            pass_on(below(d), d + 1, 1, unit)
            z_copy(above(d), 0, unit).wait_recv()
            pass_on(above(d), d + 1, 0, unit)

    scaling = math.log2(math.e) * D ** (-0.5)

    def key_positions(planes, pieces):
        count = len(pieces) * len(planes) * Y * C * R
        lane = lax.broadcasted_iota(jnp.int32, (1, count), 1)
        segment = lane // R
        total = lane % R
        at = 0
        for piece in pieces:
            for plane in planes:
                for yy in range(Y):
                    for cc in range(C):
                        slot = cc * (Z * Y) + plane * Y + yy
                        total = total + jnp.where(segment == at, first_pos(slot, piece), 0)
                        at += 1
        return total

    def query_positions(piece, yy, cc):
        row = lax.broadcasted_iota(jnp.int32, (R, D), 0)
        return row + first_pos(cc * (Z * Y) + z * Y + yy, piece)

    for piece in range(X):
        for yy in range(Y):
            for cc in range(C):
                pos_ref[piece, yy, cc] = query_positions(piece, yy, cc)

    early = list(range(X // 2))
    late = list(range(X // 2, X))

    def attend(planes, pieces_here, first, last):

        def units(kind, head, pieces):
            return jnp.concatenate(
                [
                    kv_all[plane, p, yy, cc, kind, head]
                    for p in pieces
                    for plane in planes
                    for yy in range(Y)
                    for cc in range(C)
                ],
                axis=0,
            )

        if planes:
            key_pos = {"early": key_positions(planes, early), "late": key_positions(planes, late)}
        def blocks_of(step, unused):
            dy = Y - 1 - step
            yy = (y + dy) % Y
            for piece in pieces_here:
                own = "early" if piece in early else "late"
                parts = ["early"] if own == "early" else ["early", "late"]
                for head in range(KVL):
                    if planes:
                        query = q_all[piece, head, yy].reshape(rows, D)
                        scores = [
                            lax.dot_general(
                                query,
                                units(0, head, early if part == "early" else late),
                                (((1,), (1,)), ((), ())),
                                preferred_element_type=jnp.float32,
                            )
                            for part in parts
                        ]
                        width = math.gcd(scores[0].shape[1], D)
                        rounded, totals, factors = [], [], []
                        for at in range(0, rows, R):
                            block = slice(at, at + R)
                            seen_to = pos_ref[piece, yy, at // (G * R), :, :width]
                            columns = []
                            for part, s in zip(parts, scores):
                                for start in range(0, s.shape[1], width):
                                    column = s[block, start : start + width]
                                    if part == own:
                                        seen = key_pos[part][:, start : start + width] <= seen_to
                                        column = jnp.where(seen, column, mask_floor)
                                    columns.append(column)
                            top = jnp.max(
                                functools.reduce(jnp.maximum, columns), axis=-1, keepdims=True
                            )
                            top = jnp.broadcast_to(top, (R, D))
                            if not first:
                                before = max_ref[piece, head, yy, block]
                                top = jnp.maximum(top, before)
                                factors.append(jnp.exp2((before - top) * scaling))
                            weights = [jnp.exp2((s - top[:, :width]) * scaling) for s in columns]
                            total = sum(weights)
                            if width < D:
                                filler = jnp.zeros((R, D - width), total.dtype)
                                total = jnp.concatenate([total, filler], axis=1)
                            if not first:
                                total = total + sum_ref[piece, head, yy, block] * factors[-1]
                            totals.append(total)
                            rounded.append([w.astype(jnp.bfloat16) for w in weights])
                            if not last:
                                max_ref[piece, head, yy, block] = top
                        weights = [jnp.concatenate(ws, axis=0) for ws in zip(*rounded)]
                        if width == D:
                            weights = [jnp.concatenate(weights, axis=1)]
                        total = jnp.concatenate(totals, axis=0)
                        shared = units(1, head, early if own == "early" else early + late)
                        update, start = 0.0, 0
                        for w in weights:
                            update = update + jnp.dot(
                                w,
                                shared[start : start + w.shape[1]],
                                preferred_element_type=jnp.float32,
                            )
                            start += w.shape[1]
                        if not first:
                            factor = jnp.concatenate(factors, axis=0)
                            update = update + acc_ref[piece, head, yy] * factor
                    else:
                        total, update = sum_ref[piece, head, yy], acc_ref[piece, head, yy]
                    if last:
                        mixed = update * (1.0 / jnp.sum(total, axis=-1, keepdims=True))
                        out_part[piece, yy, :, head] = mixed.astype(jnp.bfloat16).reshape(
                            C, G, R, D
                        )
                    else:
                        sum_ref[piece, head, yy] = total
                        acc_ref[piece, head, yy] = update
                if last:
                    for dc in range(1, C):
                        o_copy(dy, dc, piece).start()

                    def keep():
                        out_ref[y * C + c, :, :, pl.ds(piece * R, R)] = out_part[piece, y, c]

                    pl.when(dy > 0)(lambda: o_copy(dy, 0, piece).start())
                    pl.when(dy == 0)(keep)
            return unused

        lax.fori_loop(0, Y, blocks_of, 0)

    def o_copy(dy, dc, piece):
        xx, yy, cc = member(0, dy, dc)
        return remote(
            out_part.at[piece, yy, cc],
            out_ref.at[y * C + c, :, :, pl.ds(piece * R, R)],
            o_send.at[dy, dc, piece],
            o_recv.at[dy, dc, piece],
            device(x, cc, z * Y + yy),
        )

    if whole_way > 0:
        receive(1)
    for offset in offsets:
        q_copy(*offset).wait_recv()
    attend([z] + [below(1), above(1)] * min(1, whole_way), range(X), True, Z == 1)

    def later(d):
        receive(d)
        attend([below(d), above(d)], range(X), False, False)

    small_loop(2, whole_way + 1, later)
    if Z % 2 == 0:
        opposite = above(Z // 2)
        for pieces in (early, late):
            for j, unit in enumerate(units_sorted):
                if j // Y in pieces:
                    z_copy(opposite, 1, unit).wait_recv()
            attend([opposite], pieces, False, True)
    elif Z > 1:
        attend([], range(X), False, True)

    for offset in offsets:
        kv_copy(*offset).wait_send()
        q_copy(*offset).wait_send()
    def sent(d):
        for j, unit in enumerate(units_sorted):
            z_copy(below(d), 1, unit).wait_send()
            z_copy(above(d), 0, unit).wait_send()

    small_loop(0, whole_way, sent)
    if Z % 2 == 0:
        for j, unit in enumerate(units_sorted):
            pl.when(z % 2 == 0)(lambda: z_copy(below(Z // 2 - 1), 1, unit).wait_send())
            pl.when(z % 2 == 1)(lambda: z_copy(above(Z // 2 - 1), 0, unit).wait_send())
    for dx, dy, dc in offsets:
        if dx == 0:
            for piece in range(X):
                o_copy(dy, dc, piece).wait()


def per_device(queries, keys, values, run_index):
    X, C, B = lax.axis_size("heads"), lax.axis_size("team"), lax.axis_size("blk")
    R, QH, D = queries.shape[1:]
    KVH = keys.shape[2]
    Y = math.gcd(KVH // (X * C), B)
    KVL = KVH // (X * C * Y)
    G = QH // KVH
    Z = B // Y
    freqs = inverse_freqs(D)
    freqs = jnp.asarray(np.concatenate([freqs, freqs])[None], jnp.float32)
    rows = C * G * R
    hbm = pl.BlockSpec(memory_space=pltpu.HBM)
    dma = pltpu.SemaphoreType.DMA
    bf16, f32 = jnp.bfloat16, jnp.float32
    out = pl.pallas_call(
        functools.partial(attend_kernel, (X, C, Z, Y, R, KVL, G, D)),
        out_shape=pltpu.VMEM((Y * C, KVL, G, X * R, D), bf16),
        in_specs=[hbm] * 5,
        out_specs=pl.BlockSpec(memory_space=pltpu.VMEM),
        scratch_shapes=[
            pltpu.SMEM(run_index.shape, run_index.dtype),
            pltpu.VMEM(freqs.shape, f32),
            pltpu.VMEM(queries.shape, bf16),
            pltpu.VMEM(keys.shape, bf16),
            pltpu.VMEM(values.shape, bf16),
            dma((5,)),
            pltpu.VMEM((X * Y * C, 2, KVL, R, D), bf16),
            pltpu.VMEM((X * Y * C, KVL, G, R, D), bf16),
            pltpu.VMEM((Z, X, Y, C, 2, KVL, R, D), bf16),
            pltpu.VMEM((X, KVL, Y, C, G, R, D), bf16),
            pltpu.VMEM((X, KVL, Y, rows, D), f32),
            pltpu.VMEM((X, KVL, Y, rows, D), f32),
            pltpu.VMEM((X, KVL, Y, rows, D), f32),
            pltpu.VMEM((X, Y, C, R, D), jnp.int32),
            pltpu.VMEM((X, Y, C, KVL, G, R, D), bf16),
            dma((X, Y, C)),
            dma((X, Y, C)),
            dma((X, Y, C)),
            dma((X, Y, C)),
            dma((2, Z, X, Y)),
            dma((Z, X, Y)),
            dma((Y, C, X)),
            dma((Y, C, X)),
        ],
        compiler_params=pltpu.CompilerParams(
            collective_id=0, has_side_effects=True, vmem_limit_bytes=60 * 2**20
        ),
    )(run_index, freqs, queries, keys, values)
    return jnp.transpose(out.reshape(Y * C * KVL * G, X * R, D), (1, 0, 2))


def solution(mesh):
    in_specs = (
        P("heads", ("team", "blk"), None, None),
        P("heads", ("team", "blk"), None, None),
        P("heads", ("team", "blk"), None, None),
        P(),
    )
    out_specs = P(("team", "blk"), "heads", None)
    return jax.shard_map(
        per_device, mesh=mesh, in_specs=in_specs, out_specs=out_specs, check_vma=False
    )
```
